512 devices in a mesh: section: 64 (over y_lo, z, x), tensor: 8 (over y_hi, core).
Axes of the slice: x: 4, y: 8 (y_hi: 4, y_lo: 2; y = y_hi * 2 + y_lo), z: 8, core: 2. Of those that a mesh axis runs over, the one named last changes fastest.
Arguments:
- outgoing: bfloat16 [16384, 512], P('section'), may hold values from -6 to 6
- returning: bfloat16 [16384, 512], P('section'), may hold values from -6 to 6
- token_ids: int32 [16384], P('section'), may hold values from 0 to 65535
- shared_basis: bfloat16 [512, 8192], P('section'), may hold values from -0.25 to 0.25
- embed_table: bfloat16 [8192, 65536], P(('tensor', 'section')), may hold values from -41 to 41
- norm_gain: float32 [64, 8192], P('section'), may hold values from 0.1 to 1.9
- value_weight: bfloat16 [64, 8192, 1024], P('section', None, 'tensor'), may hold values from -1 to 1
- write_basis: bfloat16 [64, 1024, 512], P('section', 'tensor'), may hold values from -2 to 2
- head_logits: bfloat16 [64, 8, 256, 256], P('section', 'tensor'), may hold values from -4 to 306, as said below
Outputs:
- next_outgoing: bfloat16 [16384, 512], P('section')
- next_returning: bfloat16 [16384, 512], P('section')
- grad_write_basis: float32 [64, 1024, 512], P('section', 'tensor')
- grad_norm_gain: bfloat16 [64, 8192], P('section')
The draws below stay inside these ranges and needn't reach their ends.
Inputs may be any that keep to these rules, and one draw needn't show every extreme that they name: `head_logits`: entries above the diagonal are not read.
All inputs are finite; a program needn't handle non-finite values.
Results may differ from the reference program's by a relative error of at most 0.018.
Values may be sent and summed in bfloat16 or wider, within the bound.
A program may use at most 128 MiB of HBM per device.

```python
import math
import jax
import jax.numpy as jnp
import numpy as np
from jax import lax

D = 8192
KVH = 8
HD = 128
R = 512
VOCAB = 65536
TOK = 256
KVW = 1024
LAYERS = 64
ROWS = 16384


def draw_embed_table(key, part):
    key = jax.random.fold_in(key, 11)
    keys = jax.random.split(key, 3)
    feature_scale = jnp.exp(jax.random.uniform(keys[0], (D, 1), jnp.float32) * jnp.log(3.16))
    token_scale = jnp.exp(jax.random.uniform(keys[1], (1, VOCAB), jnp.float32) * jnp.log(3.16))
    base = jax.random.truncated_normal(keys[2], -4.0, 4.0, (D, VOCAB), jnp.float32)
    values = base * feature_scale * token_scale
    return values.astype(jnp.bfloat16)


def draw_returning(key, part):
    key = jax.random.fold_in(key, 31)
    values = jax.random.truncated_normal(key, -6.0, 6.0, (ROWS, R), jnp.float32)
    return values.astype(jnp.bfloat16)


def draw_value_weight(key, part):
    key = jax.random.fold_in(key, 41)
    shape = (LAYERS, D, KVW)
    values = jax.random.truncated_normal(key, -6.0, 6.0, shape, jnp.float32) * D ** (-0.5)
    return values.astype(jnp.bfloat16)


def draw_write_basis(key, part):
    key = jax.random.fold_in(key, 53)
    shape = (LAYERS, KVW, R)
    values = jax.random.truncated_normal(key, -6.0, 6.0, shape, jnp.float32) * HD ** (-0.5)
    return values.astype(jnp.bfloat16)


def draw_head_logits(key, part):
    key = jax.random.fold_in(key, 23)
    keys = jax.random.split(key, 1)
    shape = (LAYERS, KVH, TOK, TOK)
    values = 1.5 * jax.random.truncated_normal(keys[0], -2.6, 2.6, shape, jnp.float32)
    return values.astype(jnp.bfloat16)


def with_ends(entries, key, least, high):
    place = [jax.random.randint(jax.random.fold_in(key, axis), (), 0, length) for axis, length in enumerate(entries.shape)]
    longest = entries.shape.index(max(entries.shape))
    neighbour = place[:longest] + [(place[longest] + 1) % entries.shape[longest]] + place[longest + 1:]
    return entries.at[tuple(place)].set(least).at[tuple(neighbour)].set(high)


def levels(own_key, extent, cuts, least, top_value):
    loudness = 1.0
    for position, shards_of in cuts:
        steps = jax.random.uniform(jax.random.fold_in(jax.random.fold_in(own_key, 6), position), (shards_of,), jnp.float32, least / len(cuts), top_value / len(cuts))
        loudness = loudness * jnp.repeat(jnp.exp(steps), extent[position] // shards_of).reshape((-1,) + (1,) * (len(extent) - 1 - position))
    return loudness


def rank_table(count, slope):
    weights = [(1 << 20) // math.isqrt(rank ** slope) + 1 for rank in range(1, count + 1)]
    scale = 1 + sum(weights) // (1 << 30)
    return np.cumsum(np.array([max(1, weight // scale) for weight in weights]))


def ranked_ids(own_key, shape, number_of, skew):
    grid = rank_table(number_of, skew)
    lot = jax.random.randint(jax.random.fold_in(own_key, 1), shape, 0, int(grid[number_of - 1]))
    standing = jnp.searchsorted(jnp.asarray(grid, jnp.int32), lot, side="right")
    return jax.random.permutation(jax.random.fold_in(own_key, 2), number_of)[standing].astype(jnp.int32)


def centred(rng, extent, deviation, reach, cuts=(), dtype=jnp.bfloat16):
    drawn = jax.random.normal(rng, extent, jnp.float32) * deviation
    if len(cuts) > 0:
        drawn = levels(rng, extent, cuts, -0.22, 0.18) * drawn
    return jnp.clip(drawn, min=-reach, max=reach).astype(dtype)


def setup_inputs(seed: int = 0) -> dict:
    splits = jax.random.split(jax.random.key(seed), 10)
    return {
        "outgoing": centred(splits[0], (ROWS, R), 1.0, 6.0, ((0, 64),)),
        "returning": draw_returning(jax.random.fold_in(splits[9], 71), 0),
        "token_ids": with_ends(ranked_ids(splits[2], (ROWS,), VOCAB, 2), jax.random.fold_in(splits[2], 3), 0, VOCAB - 1).astype(jnp.int32),
        "shared_basis": centred(splits[3], (R, D), R ** -0.5, 0.25, ((0, 64),)),
        "embed_table": draw_embed_table(jax.random.fold_in(splits[9], 71), 0),
        "norm_gain": jnp.clip(1.0 + 0.18 * jax.random.normal(splits[5], (LAYERS, D), jnp.float32), 0.1, 1.9),
        "value_weight": draw_value_weight(jax.random.fold_in(splits[9], 71), 0),
        "write_basis": draw_write_basis(jax.random.fold_in(splits[9], 71), 0),
        "head_logits": draw_head_logits(jax.random.fold_in(splits[9], 71), 0),
    }


def section_step(coef_in, cotangent, section_ids, norm_gain, value_weight, write_basis, head_logits, shared_basis, embed_table):
    embedded = jnp.take(embed_table, section_ids, axis=1).T.astype(jnp.float32)
    rebuilt = (jnp.dot(coef_in, shared_basis, preferred_element_type=jnp.float32) + embedded).astype(jnp.bfloat16)
    residual = rebuilt.astype(jnp.float32)
    spread = jnp.sqrt(lax.optimization_barrier(jnp.mean(residual * residual, axis=-1, keepdims=True)) + 1e-05)
    normed = (residual / spread * norm_gain[None, :]).astype(jnp.bfloat16)
    values = jnp.dot(normed, value_weight, preferred_element_type=jnp.float32).astype(jnp.bfloat16)
    value_heads = values.reshape(TOK, KVH, HD)
    causal = jnp.arange(TOK)[:, None] >= jnp.arange(TOK)[None, :]
    scores = jnp.where(causal[None], head_logits.astype(jnp.float32), -1e+30)
    highest = lax.optimization_barrier(jnp.max(scores, axis=-1, keepdims=True))
    weights = jnp.exp(scores - highest)
    head_weights = (weights / lax.optimization_barrier(jnp.sum(weights, axis=-1, keepdims=True))).astype(jnp.bfloat16)
    attended = jnp.einsum('hqk,khd->qhd', head_weights.astype(jnp.float32), value_heads.astype(jnp.float32))
    attended = attended.astype(jnp.bfloat16).reshape(TOK, KVW)
    delta = jnp.dot(attended, write_basis, preferred_element_type=jnp.float32)
    next_outgoing = (coef_in.astype(jnp.float32) + delta).astype(jnp.bfloat16)
    grad_write = jnp.dot(attended.T, cotangent, preferred_element_type=jnp.float32)
    grad_attended = jnp.dot(cotangent, write_basis.T, preferred_element_type=jnp.float32).astype(jnp.bfloat16)
    grad_values = jnp.einsum('hqk,qhd->khd', head_weights.astype(jnp.float32), grad_attended.reshape(TOK, KVH, HD).astype(jnp.float32))
    grad_values = grad_values.astype(jnp.bfloat16).reshape(TOK, KVW)
    grad_normed = jnp.dot(grad_values, value_weight.T, preferred_element_type=jnp.float32)
    grad_gain = lax.optimization_barrier(jnp.sum(grad_normed * residual / spread, axis=0)).astype(jnp.bfloat16)
    inner_sum = lax.optimization_barrier(jnp.sum(grad_normed * norm_gain[None, :] * residual, axis=-1, keepdims=True))
    grad_rebuilt = norm_gain[None, :] * grad_normed / spread - residual * inner_sum / (D * spread ** 3)
    grad_coef = jnp.dot(grad_rebuilt, shared_basis.astype(jnp.float32).T, precision=lax.Precision.HIGHEST)
    next_returning = (cotangent.astype(jnp.float32) + grad_coef).astype(jnp.bfloat16)
    return (next_outgoing, next_returning, grad_write, grad_gain)

def reference(outgoing, returning, token_ids, shared_basis, embed_table, norm_gain, value_weight, write_basis, head_logits):
    sent_sections = outgoing.reshape(LAYERS, TOK, R)
    back_sections = returning.reshape(LAYERS, TOK, R)
    coef_in = jnp.concatenate([jnp.zeros_like(sent_sections[:1]), sent_sections[:-1]], axis=0)
    cotangent = jnp.concatenate([back_sections[1:], back_sections[-1:]], axis=0)
    section_ids = token_ids.reshape(LAYERS, TOK)

    def one_section(inputs):
        return section_step(*inputs, shared_basis, embed_table)
    results = lax.map(one_section, (coef_in, cotangent, section_ids, norm_gain, value_weight, write_basis, head_logits))
    return (results[0].reshape(ROWS, R), results[1].reshape(ROWS, R), results[2], results[3])
```

```python
import functools

import jax
import jax.numpy as jnp
from jax import lax
from jax.experimental import pallas as pl
from jax.experimental.pallas import tpu as pltpu
from jax.sharding import PartitionSpec as P

D = 8192
HD = 128
R = 512
TOK = 256
VOCAB = 65536
FEAT = 16
NS = 64
NT = 8
WIDTH = FEAT * NS
ROWS = TOK // NT
MESH = pl.DeviceIdType.MESH
F32 = jnp.float32
BF16 = jnp.bfloat16


def dot(a, b):
    return jnp.dot(a, b, preferred_element_type=F32)


def dot_nt(a, b):
    return lax.dot_general(a, b, (((1,), (1,)), ((), ())), preferred_element_type=F32)


def wait_bytes(view, sem):
    pltpu.make_async_copy(view, view, sem).wait()


def kernel(
    outgoing, returning, ids, basis_own, table, gain, weight, write, logits,
    next_out, next_ret, grad_write, grad_gain,
    ids_own, ids_all, ids_scalar, coef, cot, piece, pieces, basis, w_all, table_t, stage,
    emb_out, emb_in, gv_own, gv_all, heads, gn, res_c, res, ng, sq_acc, in_acc,
    v_out, v_in, st_out, st_in, g_hi, g_lo, rs_out, rs_in, ag_own, ag_in, gg_own, gg_in,
    send, recv, local,
):
    s = lax.axis_index("section")
    t = lax.axis_index("tensor")

    def section_peer(k):
        return lax.rem(s + k, NS)

    def tensor_peer(k):
        return lax.rem(t + k, NT)

    own = ids[...]
    ids_own[0:2, :] = (own >> 10) * 128 + (own & 127)
    ids_own[2:4, :] = (own >> 7) & 7
    part = basis_own[:, pl.ds(pl.multiple_of(t * WIDTH, WIDTH), WIDTH)].astype(F32)
    piece[...] = jnp.concatenate([part[:, : WIDTH // 2], part[:, WIDTH // 2 :]], axis=0).astype(BF16)

    barrier = pltpu.get_barrier_semaphore()

    def greet_section(k, c):
        pl.semaphore_signal(barrier, inc=1, device_id=(section_peer(k), t), device_id_type=MESH)
        return c

    def greet_tensor(k, c):
        pl.semaphore_signal(barrier, inc=1, device_id=(s, tensor_peer(k)), device_id_type=MESH)
        return c

    lax.fori_loop(1, NS, greet_section, 0)
    lax.fori_loop(1, NT, greet_tensor, 0)
    pl.semaphore_wait(barrier, NS + NT - 2)

    def to_section(src, dst, which, p):
        pltpu.make_async_remote_copy(
            src_ref=src, dst_ref=dst, send_sem=send.at[which], recv_sem=recv.at[which],
            device_id=(p, t), device_id_type=MESH,
        ).start()

    def to_tensor(src, dst, which, p):
        pltpu.make_async_remote_copy(
            src_ref=src, dst_ref=dst, send_sem=send.at[which], recv_sem=recv.at[which],
            device_id=(s, p), device_id_type=MESH,
        ).start()

    def send_ids(k, c):
        to_section(ids_own, ids_all.at[s], 0, section_peer(k))
        return c

    lax.fori_loop(1, NS, send_ids, 0)
    ids_all[s] = ids_own[...]
    to_section(outgoing, coef, 1, section_peer(1))
    to_section(returning, cot, 2, section_peer(NS - 1))

    own_cols = pl.ds(pl.multiple_of(t * HD, HD), HD)

    def send_weight(k, c):
        p = tensor_peer(k)
        to_tensor(weight.at[0, pl.ds(pl.multiple_of(p * WIDTH, WIDTH), WIDTH)], w_all.at[:, own_cols], 4, p)
        return c

    lax.fori_loop(1, NT, send_weight, 0)
    w_here = pltpu.make_async_copy(
        weight.at[0, pl.ds(pl.multiple_of(t * WIDTH, WIDTH), WIDTH)], w_all.at[:, own_cols], local.at[0]
    )
    w_here.start()

    def send_basis(k, c):
        to_section(piece, pieces.at[s], 3, section_peer(k))
        return c

    lax.fori_loop(1, NS, send_basis, 0)
    pieces[s] = piece[...]

    def turn(b, c):
        x = table[:, pl.ds(pl.multiple_of(b * 1024, 1024), 1024)]
        x = jnp.concatenate([x[:, v * 128 : (v + 1) * 128] for v in range(8)], axis=0)
        table_t[pl.ds(pl.multiple_of(b * 128, 128), 128), :] = x.astype(F32).T
        return c

    lax.fori_loop(0, VOCAB // 1024, turn, 0)

    query = lax.broadcasted_iota(jnp.int32, (TOK, TOK), 0)
    key = lax.broadcasted_iota(jnp.int32, (TOK, TOK), 1)
    scores = jnp.where(query >= key, logits[0, 0].astype(F32), -1e30)
    expd = jnp.exp(scores - jnp.max(scores, axis=1, keepdims=True))
    soft = expd / jnp.sum(expd, axis=1, keepdims=True)
    heads[...] = soft.astype(BF16)
    to_turn = soft.T.astype(BF16)
    wait_bytes(cot, recv.at[2])

    @pl.when(s == NS - 1)
    def _():
        cot[...] = returning[...]

    ga = dot_nt(cot[...], write[0]).astype(BF16)
    gv_own[...] = dot(to_turn, ga).astype(BF16)

    def send_gv(k, c):
        to_tensor(gv_own, gv_all.at[:, own_cols], 5, tensor_peer(k))
        return c

    lax.fori_loop(1, NT, send_gv, 0)
    gv_all[:, own_cols] = gv_own[...]

    wait_bytes(ids_all.at[pl.ds(0, NS - 1)], recv.at[0])
    scalar_copy = pltpu.make_async_copy(ids_all, ids_scalar, local.at[1])
    scalar_copy.start()
    scalar_copy.wait()
    lane = lax.broadcasted_iota(jnp.int32, (8, 128), 1)
    sub = lax.broadcasted_iota(jnp.int32, (8, 128), 0)
    group = lane // FEAT

    def find(p, half):
        groups = jnp.broadcast_to(ids_all[p, pl.ds(2 + half, 1), :], (8, 128))
        for j in range(128):
            stage[pl.ds(j, 1), :] = table_t[pl.ds(ids_scalar[p, half, j], 1), :]
        outs = []
        for q in range(2):
            place = jnp.take_along_axis(groups, 16 * group + 8 * q + sub, axis=1) * FEAT + lane % FEAT
            acc = None
            for b in range(8):
                x = jnp.take_along_axis(stage[16 * b + 8 * q : 16 * b + 8 * q + 8, :], place, axis=1)
                acc = x if acc is None else jnp.where(group == b, x, acc)
            outs.append(acc)
        return jnp.concatenate(outs, axis=0).astype(BF16)

    def look_up(k, c):
        p = section_peer(k)

        def one_half(half, cc):
            emb_out[p, pl.ds(pl.multiple_of(half * 16, 16), 16), :] = find(p, half)
            return cc

        lax.fori_loop(0, 2, one_half, 0)

        to_section(emb_out.at[p], emb_in.at[s], 6, p)
        return c

    lax.fori_loop(1, NS, look_up, 0)

    def own_half(half, c):
        emb_in[s, pl.ds(pl.multiple_of(half * 16, 16), 16), :] = find(s, half)
        return c

    lax.fori_loop(0, 2, own_half, 0)

    wait_bytes(coef, recv.at[1])

    @pl.when(s == 0)
    def _():
        coef[...] = jnp.zeros_like(coef)

    wait_bytes(pieces.at[pl.ds(0, NS - 1)], recv.at[3])

    def order(i, c):
        x = pieces[pl.ds(i * 8, 8)].astype(F32)
        rows = pl.ds(pl.multiple_of(i * 64, 64), 64)
        for h in range(2):
            basis[rows, h * 512 : (h + 1) * 512] = x[:, 8 * h : 8 * h + 8, :].reshape(64, 512).astype(BF16)
        return c

    lax.fori_loop(0, NS // 8, order, 0)
    res_c[...] = dot(coef[...], basis[...])

    w_here.wait()
    wait_bytes(w_all.at[:, pl.ds(0, (NT - 1) * HD)], recv.at[4])
    wait_bytes(gv_all.at[:, pl.ds(0, (NT - 1) * HD)], recv.at[5])
    gn[...] = dot_nt(gv_all[...], w_all[...])

    wait_bytes(emb_in.at[pl.ds(0, NS - 1)], recv.at[6])
    sq_acc[...] = jnp.zeros_like(sq_acc)
    in_acc[...] = jnp.zeros_like(in_acc)
    lane16 = lax.broadcasted_iota(jnp.int32, (16, 128), 1) // FEAT

    def gain_row(u):
        return gain[:, pl.ds(pl.multiple_of(t * WIDTH + u * 128, 128), 128)]

    def assemble(u, c):
        cols = pl.ds(pl.multiple_of(u * 128, 128), 128)
        g_row = gain_row(u)
        for half in range(2):
            x = [emb_in[8 * u + v, 16 * half : 16 * half + 16, :].astype(F32) for v in range(8)]
            for d in (4, 2, 1):
                low = (lane16 & d) == 0
                y = list(x)
                for v in range(8):
                    if v & d == 0:
                        a, b = x[v], x[v + d]
                        y[v] = jnp.where(low, a, pltpu.roll(b, 16 * d, 1))
                        y[v + d] = jnp.where(low, pltpu.roll(a, 128 - 16 * d, 1), b)
                x = y
            for b in range(8):
                rows = slice(128 * half + 16 * b, 128 * half + 16 * b + 16)
                r = (res_c[rows, cols] + x[b]).astype(BF16)
                res[rows, cols] = r
                r = r.astype(F32)
                scaled = r * g_row
                ng[rows, cols] = scaled.astype(BF16)
                sq_acc[rows, :] += r * r
                in_acc[rows, :] += gn[rows, cols] * scaled
        return c

    lax.fori_loop(0, WIDTH // 128, assemble, 0)
    st_out[...] = jnp.zeros_like(st_out)
    st_out[0:1, :] = jnp.sum(sq_acc[...].T, axis=0, keepdims=True)
    st_out[1:2, :] = jnp.sum(in_acc[...].T, axis=0, keepdims=True)

    def send_stats(k, c):
        to_tensor(st_out, st_in.at[t], 8, tensor_peer(k))
        return c

    lax.fori_loop(1, NT, send_stats, 0)
    st_in[t] = st_out[...]
    for h in range(NT // 2):
        v = dot(ng[...], w_all[:, h * 256 : (h + 1) * 256]).astype(BF16)
        v_out[2 * h] = v[:, :HD]
        v_out[2 * h + 1] = v[:, HD:]

    def send_values(k, c):
        p = tensor_peer(k)
        to_tensor(v_out.at[p], v_in.at[t], 7, p)
        return c

    lax.fori_loop(1, NT, send_values, 0)
    v_in[t] = v_out[t]

    wait_bytes(st_in.at[pl.ds(0, NT - 1)], recv.at[8])
    total = st_in[0]
    for i in range(1, NT):
        total = total + st_in[i]
    spread = jnp.sqrt(total[0:1, :] / D + 1e-5)
    inv_row = 1.0 / spread
    back_row = total[1:2, :] * inv_row * inv_row * inv_row / D
    inv = jnp.broadcast_to(inv_row, (128, TOK)).T
    back = jnp.broadcast_to(back_row, (128, TOK)).T
    for u in range(WIDTH // 128):
        cols = slice(u * 128, (u + 1) * 128)
        n = gn[:, cols] * inv
        r = res[:, cols].astype(F32)
        gg_own[u : u + 1, :] = jnp.sum(n * r, axis=0, keepdims=True)
        g = n * gain_row(u) - r * back
        upper = g.astype(BF16)
        g_hi[:, cols] = upper
        g_lo[:, cols] = (g - upper.astype(F32)).astype(BF16)

    def send_gain(k, c):
        to_tensor(gg_own, gg_in.at[t], 11, tensor_peer(k))
        return c

    lax.fori_loop(1, NT, send_gain, 0)
    gg_in[t] = gg_own[...]
    grad = (dot_nt(g_hi[...], basis[...]) + dot_nt(g_lo[...], basis[...])).astype(BF16)
    for i in range(NT):
        rs_out[i, ROWS : 2 * ROWS, :] = grad[i * ROWS : (i + 1) * ROWS, :]

    wait_bytes(v_in.at[pl.ds(0, NT - 1)], recv.at[7])
    v = v_in[0].astype(F32)
    for i in range(1, NT):
        v = v + v_in[i].astype(F32)
    values = (v * inv).astype(BF16)
    attended = dot(heads[...], values)
    att = attended.astype(BF16)
    delta = dot(att, write[0]).astype(BF16)
    for i in range(NT):
        rs_out[i, 0:ROWS, :] = delta[i * ROWS : (i + 1) * ROWS, :]

    def send_rows(k, c):
        p = tensor_peer(k)
        to_tensor(rs_out.at[p], rs_in.at[t], 9, p)
        return c

    lax.fori_loop(1, NT, send_rows, 0)
    rs_in[t] = rs_out[t]
    grad_write[...] = dot(att.astype(F32).T.astype(BF16), cot[...])

    wait_bytes(rs_in.at[pl.ds(0, NT - 1)], recv.at[9])
    total = rs_in[0].astype(F32)
    for i in range(1, NT):
        total = total + rs_in[i].astype(F32)
    mine = pl.ds(pl.multiple_of(t * ROWS, ROWS), ROWS)
    ag_own[0:ROWS, :] = (coef[mine, :].astype(F32) + total[0:ROWS, :]).astype(BF16)
    ag_own[ROWS : 2 * ROWS, :] = (cot[mine, :].astype(F32) + total[ROWS : 2 * ROWS, :]).astype(BF16)

    def send_sums(k, c):
        to_tensor(ag_own, ag_in.at[t], 10, tensor_peer(k))
        return c

    lax.fori_loop(1, NT, send_sums, 0)
    ag_in[t] = ag_own[...]
    wait_bytes(gg_in.at[pl.ds(0, NT - 1)], recv.at[11])
    grad_gain[...] = jnp.concatenate(
        [gg_in[i, j : j + 1, :] for i in range(NT) for j in range(8)], axis=1
    ).astype(BF16)
    wait_bytes(ag_in.at[pl.ds(0, NT - 1)], recv.at[10])
    for i in range(NT):
        next_out[i * ROWS : (i + 1) * ROWS, :] = ag_in[i, 0:ROWS, :]
        next_ret[i * ROWS : (i + 1) * ROWS, :] = ag_in[i, ROWS : 2 * ROWS, :]

    wait_bytes(ids_all.at[pl.ds(0, NS - 1)], send.at[0])
    wait_bytes(coef, send.at[1])
    wait_bytes(cot, send.at[2])
    wait_bytes(pieces.at[pl.ds(0, NS - 1)], send.at[3])
    wait_bytes(w_all.at[:, pl.ds(0, (NT - 1) * HD)], send.at[4])
    wait_bytes(gv_all.at[:, pl.ds(0, (NT - 1) * HD)], send.at[5])
    wait_bytes(emb_in.at[pl.ds(0, NS - 1)], send.at[6])
    wait_bytes(v_in.at[pl.ds(0, NT - 1)], send.at[7])
    wait_bytes(st_in.at[pl.ds(0, NT - 1)], send.at[8])
    wait_bytes(rs_in.at[pl.ds(0, NT - 1)], send.at[9])
    wait_bytes(ag_in.at[pl.ds(0, NT - 1)], send.at[10])
    wait_bytes(gg_in.at[pl.ds(0, NT - 1)], send.at[11])


def shards(
    outgoing, returning, token_ids, shared_basis, embed_table, norm_gain, value_weight, write_basis, head_logits
):
    vmem = pl.BlockSpec(memory_space=pltpu.VMEM)
    hbm = pl.BlockSpec(memory_space=pl.ANY)
    next_out, next_ret, grad_write, grad_gain = pl.pallas_call(
        kernel,
        out_shape=(
            jax.ShapeDtypeStruct((TOK, R), BF16),
            jax.ShapeDtypeStruct((TOK, R), BF16),
            jax.ShapeDtypeStruct((HD, R), F32),
            jax.ShapeDtypeStruct((1, D), BF16),
        ),
        in_specs=[vmem, vmem, vmem, vmem, vmem, vmem, hbm, vmem, vmem],
        out_specs=(vmem, vmem, vmem, vmem),
        scratch_shapes=[
            pltpu.VMEM((4, 128), jnp.int32),
            pltpu.VMEM((NS, 4, 128), jnp.int32),
            pltpu.SMEM((NS, 4, 128), jnp.int32),
            pltpu.VMEM((TOK, R), BF16),
            pltpu.VMEM((TOK, R), BF16),
            pltpu.VMEM((16, WIDTH // 2), BF16),
            pltpu.VMEM((NS, 16, WIDTH // 2), BF16),
            pltpu.VMEM((R, WIDTH), BF16),
            pltpu.VMEM((WIDTH, NT * HD), BF16),
            pltpu.VMEM((VOCAB // 8, 128), F32),
            pltpu.VMEM((128, 128), F32),
            pltpu.VMEM((NS, 32, 128), BF16),
            pltpu.VMEM((NS, 32, 128), BF16),
            pltpu.VMEM((TOK, HD), BF16),
            pltpu.VMEM((TOK, NT * HD), BF16),
            pltpu.VMEM((TOK, TOK), BF16),
            pltpu.VMEM((TOK, WIDTH), F32),
            pltpu.VMEM((TOK, WIDTH), F32),
            pltpu.VMEM((TOK, WIDTH), BF16),
            pltpu.VMEM((TOK, WIDTH), BF16),
            pltpu.VMEM((TOK, 128), F32),
            pltpu.VMEM((TOK, 128), F32),
            pltpu.VMEM((NT, TOK, HD), BF16),
            pltpu.VMEM((NT, TOK, HD), BF16),
            pltpu.VMEM((8, TOK), F32),
            pltpu.VMEM((NT, 8, TOK), F32),
            pltpu.VMEM((TOK, WIDTH), BF16),
            pltpu.VMEM((TOK, WIDTH), BF16),
            pltpu.VMEM((NT, 2 * ROWS, R), BF16),
            pltpu.VMEM((NT, 2 * ROWS, R), BF16),
            pltpu.VMEM((2 * ROWS, R), BF16),
            pltpu.VMEM((NT, 2 * ROWS, R), BF16),
            pltpu.VMEM((8, 128), F32),
            pltpu.VMEM((NT, 8, 128), F32),
            pltpu.SemaphoreType.DMA((12,)),
            pltpu.SemaphoreType.DMA((12,)),
            pltpu.SemaphoreType.DMA((2,)),
        ],
        compiler_params=pltpu.CompilerParams(
            collective_id=0, has_side_effects=True, vmem_limit_bytes=52 * 2**20
        ),
        name="relay",
    )(
        outgoing, returning, token_ids.reshape(2, 128), shared_basis, embed_table, norm_gain, value_weight,
        write_basis, head_logits,
    )
    return (next_out, next_ret, grad_write[None], grad_gain)


def solution(mesh):
    placed = (
        P("section", None),
        P("section", None),
        P("section"),
        P("section", None),
        P(("tensor", "section"), None),
        P("section", None),
        P("section", None, "tensor"),
        P("section", "tensor", None),
        P("section", "tensor", None, None),
    )
    return jax.shard_map(
        shards,
        mesh=mesh,
        in_specs=placed,
        out_specs=(
            P("section", None),
            P("section", None),
            P("section", "tensor", None),
            P("section", None),
        ),
        check_vma=False,
    )
```

```python
import functools

import jax
import jax.numpy as jnp
from jax import lax
from jax.experimental import pallas as pl
from jax.experimental.pallas import tpu as pltpu
from jax.sharding import PartitionSpec as P

D = 8192
HD = 128
R = 512
TOK = 256
VOCAB = 65536
FEAT = 16
NS = 64
NT = 8
WIDTH = FEAT * NS
ROWS = TOK // NT
HALF = TOK // 2
CHIPS = 4
CHIP_W = 2 * WIDTH
NX = 4
NZ = 8
AT_Z = 12
AT_X = 36
AT_ROWS = 44
AT_GRAD = 52
MESH = pl.DeviceIdType.MESH
F32 = jnp.float32
BF16 = jnp.bfloat16


def dot(a, b):
    return jnp.dot(a, b, preferred_element_type=F32)


def dot_nt(a, b):
    return lax.dot_general(a, b, (((1,), (1,)), ((), ())), preferred_element_type=F32)


def wait_bytes(view, sem):
    pltpu.make_async_copy(view, view, sem).wait()


def kernel(
    outgoing, returning, ids, basis_hbm, table_hbm, gain_hbm, weight, write_hbm, logits_hbm,
    next_out, next_ret, grad_write, grad_gain,
    basis_own, table, gain, write, logits,
    ids_raw, ids_own, ids_all, ids_scalar, coef, cot, pieces, basis, w_all, table_t, stage,
    emb_out, emb_in, gv_own, gv_all, heads, gn, gn_in, res_c, res, ng, acc, v_out, v_in, st_out, st_in,
    in_out, in_in, g_hi, g_lo, att_own, att_in, rs_out, rs_in, ag, ag_in, gg_own, gg_in,
    send, recv, local,
):
    s = lax.axis_index("section")
    t = lax.axis_index("tensor")
    chip = t // 2
    core = lax.rem(t, 2)
    other = 1 - core
    y_lo = s // (NX * NZ)
    z = lax.rem(s // NX, NZ)
    x = lax.rem(s, NX)

    def section_peer(k):
        return lax.rem(s + k, NS)

    def tensor_peer(k):
        return lax.rem(t + k, NT)

    def chip_peer(k):
        return lax.rem(chip + k, CHIPS)

    def fetch(src, dst, which):
        copy = pltpu.make_async_copy(src, dst, local.at[which])
        copy.start()
        return copy

    ids_copy = fetch(ids, ids_raw, 0)
    basis_copy = fetch(basis_hbm.at[:, pl.ds(pl.multiple_of(t * WIDTH, WIDTH), WIDTH)], basis_own, 1)
    table_copy = fetch(table_hbm, table, 2)
    logits_copy = fetch(logits_hbm.at[0, 0], logits, 3)
    write_copy = fetch(write_hbm.at[0], write.at[core], 4)
    gain_copy = fetch(gain_hbm.at[:, pl.ds(pl.multiple_of(chip * CHIP_W, CHIP_W), CHIP_W)], gain, 5)
    chip_rows = pl.ds(pl.multiple_of(chip * CHIP_W, CHIP_W), CHIP_W)
    own_cols = pl.ds(pl.multiple_of(chip * HD, HD), HD)
    w_copy = fetch(weight.at[0, chip_rows], w_all.at[:, own_cols], 6)

    barrier = pltpu.get_barrier_semaphore()

    def greet_section(k, c):
        pl.semaphore_signal(barrier, inc=1, device_id=(section_peer(k), t), device_id_type=MESH)
        return c

    def greet_tensor(k, c):
        pl.semaphore_signal(barrier, inc=1, device_id=(s, tensor_peer(k)), device_id_type=MESH)
        return c

    lax.fori_loop(1, NS, greet_section, 0)
    lax.fori_loop(1, NT, greet_tensor, 0)

    ids_copy.wait()
    own = ids_raw[...]
    ids_own[0:2, :] = (own >> 10) * 128 + (own & 127)
    ids_own[2:4, :] = (own >> 7) & 7
    basis_copy.wait()
    part = basis_own[...].astype(F32)
    pieces[x, z, y_lo] = jnp.concatenate([part[:, : WIDTH // 2], part[:, WIDTH // 2 :]], axis=0).astype(BF16)
    pl.semaphore_wait(barrier, NS + NT - 2)

    def push(src, dst, which, peer):
        pltpu.make_async_remote_copy(
            src_ref=src, dst_ref=dst, send_sem=send.at[which], recv_sem=recv.at[which],
            device_id=peer, device_id_type=MESH,
        ).start()

    def across(k):
        return (s, chip_peer(k) * 2 + core)

    partner = (s, chip * 2 + other)

    here = pl.ds(pl.multiple_of(core * HALF, HALF), HALF)
    there = pl.ds(pl.multiple_of(other * HALF, HALF), HALF)

    def send_ids(k, c):
        push(ids_own, ids_all.at[s], 0, (section_peer(k), t))
        return c

    lax.fori_loop(1, NS, send_ids, 0)
    ids_all[s] = ids_own[...]
    push(pieces.at[x, z, y_lo], pieces.at[x, z, y_lo], 3, (lax.rem(s + NS // 2, NS), t))
    write_copy.wait()
    push(write.at[core], write.at[core], 18, partner)

    @pl.when(s > 0)
    def _():
        push(returning.at[here], cot.at[here], 2, (section_peer(NS - 1), t))

    @pl.when(s < NS - 1)
    def _():
        push(outgoing.at[here], coef.at[here], 1, (section_peer(1), t))


    table_copy.wait()

    def turn(b, c):
        tile = table[:, pl.ds(pl.multiple_of(b * 1024, 1024), 1024)]
        tile = jnp.concatenate([tile[:, v * 128 : (v + 1) * 128] for v in range(8)], axis=0)
        table_t[pl.ds(pl.multiple_of(b * 128, 128), 128), :] = tile.astype(F32).T
        return c

    lax.fori_loop(0, VOCAB // 1024, turn, 0)
    for k in (2, 1, 3):
        rows = pl.ds(pl.multiple_of(chip_peer(k) * CHIP_W, CHIP_W), CHIP_W)
        push(weight.at[0, rows], w_all.at[:, own_cols], 4, across(k))

    wait_bytes(ids_all.at[pl.ds(0, NS - 1)], recv.at[0])
    scalar_copy = fetch(ids_all, ids_scalar, 0)
    scalar_copy.wait()
    lane = lax.broadcasted_iota(jnp.int32, (8, 128), 1)
    sub = lax.broadcasted_iota(jnp.int32, (8, 128), 0)
    group = lane // FEAT

    def find(p, half):
        groups = jnp.broadcast_to(ids_all[p, pl.ds(2 + half, 1), :], (8, 128))
        for j in range(128):
            stage[pl.ds(j, 1), :] = table_t[pl.ds(ids_scalar[p, half, j], 1), :]
        outs = []
        for q in range(2):
            place = jnp.take_along_axis(groups, 16 * group + 8 * q + sub, axis=1) * FEAT + lane % FEAT
            found = None
            for b in range(8):
                row = jnp.take_along_axis(stage[16 * b + 8 * q : 16 * b + 8 * q + 8, :], place, axis=1)
                found = row if found is None else jnp.where(group == b, row, found)
            outs.append(found)
        return jnp.concatenate(outs, axis=0).astype(BF16)

    def values_gradient():
        logits_copy.wait()
        query = lax.broadcasted_iota(jnp.int32, (TOK, TOK), 0)
        key = lax.broadcasted_iota(jnp.int32, (TOK, TOK), 1)
        scores = jnp.where(query >= key, logits[...].astype(F32), -1e30)
        expd = jnp.exp(scores - jnp.max(scores, axis=1, keepdims=True))
        soft = expd / jnp.sum(expd, axis=1, keepdims=True)
        heads[...] = soft.astype(BF16)
        to_turn = soft.T.astype(BF16)

        @pl.when(s < NS - 1)
        def _():
            wait_bytes(cot.at[here], recv.at[27])

        @pl.when(s == NS - 1)
        def _():
            last = pltpu.make_async_copy(returning, cot, local.at[0])
            last.start()
            last.wait()

        ga = dot_nt(cot[...], write[core]).astype(BF16)
        gv_own[...] = dot(to_turn, ga).astype(BF16)
        for j in (2, 1, 3):
            push(gv_own, gv_all.at[:, own_cols], 5, across(j))
        gv_all[:, own_cols] = gv_own[...]

    def look_up(k, c):
        p = section_peer(k)

        def one_half(half, cc):
            emb_out[p, pl.ds(pl.multiple_of(half * 16, 16), 16), :] = find(p, half)
            return cc

        lax.fori_loop(0, 2, one_half, 0)
        push(emb_out.at[p], emb_in.at[s], 6, (p, t))

        @pl.when(k == AT_Z)
        def _():
            wait_bytes(pieces.at[0, 0, 0], recv.at[3])

            def send_z(j, cc):
                push(pieces.at[x, z], pieces.at[x, z], 11, (y_lo * NX * NZ + lax.rem(z + j, NZ) * NX + x, t))
                return cc

            lax.fori_loop(1, NZ, send_z, 0)

        @pl.when(k == AT_X)
        def _():
            wait_bytes(pieces.at[0, pl.ds(0, NZ - 1)], recv.at[11])
            for j in (2, 1, 3):
                push(pieces.at[x], pieces.at[x], 12, (y_lo * NX * NZ + z * NX + lax.rem(x + j, NX), t))

        @pl.when(jnp.logical_and(k == AT_ROWS, s < NS - 1))
        def _():
            wait_bytes(cot.at[here], recv.at[2])
            push(cot.at[here], cot.at[here], 27, partner)

        @pl.when(jnp.logical_and(k == AT_ROWS, s > 0))
        def _():
            wait_bytes(coef.at[here], recv.at[1])
            push(coef.at[here], coef.at[here], 26, partner)

        @pl.when(k == AT_GRAD)
        def _():
            values_gradient()

        return c

    lax.fori_loop(1, NS, look_up, 0)

    def own_half(half, c):
        emb_in[s, pl.ds(pl.multiple_of(half * 16, 16), 16), :] = find(s, half)
        return c

    lax.fori_loop(0, 2, own_half, 0)

    wait_bytes(pieces.at[pl.ds(0, NX - 1)], recv.at[12])
    for lo in range(2):
        for zz in range(NZ):
            tile = pieces[:, zz, lo].astype(F32)
            for xx in range(NX):
                rows = slice((lo * NZ * NX + zz * NX + xx) * 8, (lo * NZ * NX + zz * NX + xx) * 8 + 8)
                if xx % 2 == 0:
                    pair = slice(rows.start, rows.start + 16)
                    for h in range(2):
                        both = jnp.concatenate([tile[xx, 8 * h : 8 * h + 8], tile[xx + 1, 8 * h : 8 * h + 8]], axis=0)
                        basis[core, pair, h * 512 : (h + 1) * 512] = both.astype(BF16)
    push(basis.at[core], basis.at[core], 13, partner)

    @pl.when(s > 0)
    def _():
        wait_bytes(coef.at[here], recv.at[26])

    @pl.when(s == 0)
    def _():
        coef[...] = jnp.zeros_like(coef)

    res_c[...] = dot(coef[...], basis[core])

    wait_bytes(emb_in.at[pl.ds(0, NS - 1)], recv.at[6])
    acc[...] = jnp.zeros_like(acc)
    lane16 = lax.broadcasted_iota(jnp.int32, (16, 128), 1) // FEAT

    def assemble(u, c):
        cols = pl.ds(pl.multiple_of(u * 128, 128), 128)
        for half in range(2):
            xs = [emb_in[8 * u + v, 16 * half : 16 * half + 16, :].astype(F32) for v in range(8)]
            for d in (4, 2, 1):
                low = (lane16 & d) == 0
                ys = list(xs)
                for v in range(8):
                    if v & d == 0:
                        a, b = xs[v], xs[v + d]
                        ys[v] = jnp.where(low, a, pltpu.roll(b, 16 * d, 1))
                        ys[v + d] = jnp.where(low, pltpu.roll(a, 128 - 16 * d, 1), b)
                xs = ys
            for b in range(8):
                rows = slice(128 * half + 16 * b, 128 * half + 16 * b + 16)
                r = (res_c[rows, cols] + xs[b]).astype(BF16)
                res[core, rows, cols] = r
                r = r.astype(F32)
                acc[rows, :] += r * r
        return c

    lax.fori_loop(0, WIDTH // 128, assemble, 0)
    push(res.at[core], res.at[core], 14, partner)
    st_out[...] = jnp.zeros_like(st_out)
    st_out[0:1, :] = jnp.sum(acc[...].T, axis=0, keepdims=True)

    def send_squares(k, c):
        push(st_out, st_in.at[t], 8, (s, tensor_peer(k)))
        return c

    lax.fori_loop(1, NT, send_squares, 0)
    st_in[t] = st_out[...]
    wait_bytes(st_in.at[pl.ds(0, NT - 1)], recv.at[8])
    total = st_in[0]
    for i in range(1, NT):
        total = total + st_in[i]
    inv_row = 1.0 / jnp.sqrt(total[0:1, :] / D + 1e-5)
    acc[...] = jnp.broadcast_to(inv_row, (128, TOK)).T
    gain_copy.wait()
    wait_bytes(res.at[0], recv.at[14])
    for i in range(2):

        def normalise(u, c):
            cols = pl.ds(pl.multiple_of(u * 128, 128), 128)
            wide = pl.ds(pl.multiple_of(i * WIDTH + u * 128, 128), 128)
            ng[:, wide] = (res[i, :, cols].astype(F32) * acc[...] * gain[:, wide]).astype(BF16)
            return c

        lax.fori_loop(0, WIDTH // 128, normalise, 0)

    w_copy.wait()
    wait_bytes(w_all.at[:, pl.ds(0, (CHIPS - 1) * HD)], recv.at[4])
    for h in range(2):
        v = dot(ng[...], w_all[:, h * 256 : (h + 1) * 256]).astype(BF16)
        v_out[2 * h] = v[:, :HD]
        v_out[2 * h + 1] = v[:, HD:]
    for k in (2, 1, 3):
        push(v_out.at[chip_peer(k)], v_in.at[chip], 7, across(k))
    v_in[chip] = v_out[chip]

    wait_bytes(gv_all.at[:, pl.ds(0, (CHIPS - 1) * HD)], recv.at[5])
    gn[...] = dot_nt(gv_all[...], w_all[...])
    push(gn.at[there], gn_in, 15, partner)
    wait_bytes(gn_in, recv.at[15])
    inv = acc[here, :]
    inner = jnp.zeros((HALF, 128), F32)
    for u in range(CHIP_W // 128):
        cols = slice(u * 128, (u + 1) * 128)
        narrow = slice(u % 8 * 128, (u % 8 + 1) * 128)
        n = gn[here, cols] + gn_in[:, cols]
        gn_in[:, cols] = n
        r = res[u // 8, here, narrow].astype(F32)
        inner = inner + n * gain[:, cols] * r
        gg_own[u : u + 1, :] = jnp.sum(n * inv * r, axis=0, keepdims=True)
    in_out[...] = jnp.broadcast_to(jnp.sum(inner.T, axis=0, keepdims=True), (8, HALF))
    for k in (2, 1, 3):
        push(in_out, in_in.at[chip], 16, across(k))
    in_in[chip] = in_out[...]
    wait_bytes(in_in.at[pl.ds(0, CHIPS - 1)], recv.at[16])
    total = in_in[0]
    for i in range(1, CHIPS):
        total = total + in_in[i]
    back = jnp.broadcast_to(total[0:1, :], (HALF, HALF)).T * inv * inv * inv / D
    for u in range(CHIP_W // 128):
        cols = slice(u * 128, (u + 1) * 128)
        narrow = slice(u % 8 * 128, (u % 8 + 1) * 128)
        g = gn_in[:, cols] * inv * gain[:, cols] - res[u // 8, here, narrow].astype(F32) * back
        upper = g.astype(BF16)
        g_hi[u // 8, :, narrow] = upper
        g_lo[u // 8, :, narrow] = (g - upper.astype(F32)).astype(BF16)
    wait_bytes(basis.at[0], recv.at[13])
    grad = dot_nt(g_hi[0], basis[0]) + dot_nt(g_lo[0], basis[0])
    grad = grad + (dot_nt(g_hi[1], basis[1]) + dot_nt(g_lo[1], basis[1]))
    grad = grad.astype(BF16)
    for i in range(CHIPS):
        rs_out[i, ROWS : 2 * ROWS, :] = grad[i * ROWS : (i + 1) * ROWS, :]

    wait_bytes(v_in.at[pl.ds(0, CHIPS - 1)], recv.at[7])
    v = v_in[0].astype(F32)
    for i in range(1, CHIPS):
        v = v + v_in[i].astype(F32)
    attended = dot(heads[...], v.astype(BF16))
    att_own[...] = attended.astype(BF16)
    push(att_own.at[there], att_in, 17, partner)
    wait_bytes(write.at[0], recv.at[18])
    delta = dot(att_own[here, :], write[core])
    wait_bytes(att_in, recv.at[17])
    delta = (delta + dot(att_in[...], write[other])).astype(BF16)
    for i in range(CHIPS):
        rs_out[i, 0:ROWS, :] = delta[i * ROWS : (i + 1) * ROWS, :]
    for k in (2, 1, 3):
        push(rs_out.at[chip_peer(k)], rs_in.at[chip], 9, across(k))
    rs_in[chip] = rs_out[chip]

    def send_gain(k, c):
        push(gg_own, gg_in.at[t], 10, (s, tensor_peer(k)))
        return c

    lax.fori_loop(1, NT, send_gain, 0)
    gg_in[t] = gg_own[...]
    grad_write[...] = dot(attended.T.astype(BF16), cot[...])

    wait_bytes(rs_in.at[pl.ds(0, CHIPS - 1)], recv.at[9])
    total = rs_in[0].astype(F32)
    for i in range(1, CHIPS):
        total = total + rs_in[i].astype(F32)
    mine = pl.ds(pl.multiple_of(core * HALF + chip * ROWS, ROWS), ROWS)
    ag[chip, 0:ROWS, :] = (coef[mine, :].astype(F32) + total[0:ROWS, :]).astype(BF16)
    ag[chip, ROWS : 2 * ROWS, :] = (cot[mine, :].astype(F32) + total[ROWS : 2 * ROWS, :]).astype(BF16)
    for k in (2, 1, 3):
        push(ag.at[chip], ag.at[chip], 19 + k, across(k))
    push(ag.at[chip], ag_in.at[chip], 19, partner)
    wait_bytes(gg_in.at[pl.ds(0, NT - 1)], recv.at[10])
    grad_gain[...] = jnp.concatenate(
        [gg_in[2 * i, j : j + 1, :] + gg_in[2 * i + 1, j : j + 1, :] for i in range(CHIPS) for j in range(16)], axis=1
    ).astype(BF16)
    for k in (1, 3, 2):
        wait_bytes(ag.at[0], recv.at[19 + k])
        come = chip_peer(CHIPS - k)
        push(ag.at[come], ag_in.at[come], 22 + k, partner)
    for i in range(CHIPS):
        rows = pl.ds(pl.multiple_of(core * HALF + i * ROWS, ROWS), ROWS)
        next_out[rows, :] = ag[i, 0:ROWS, :]
        next_ret[rows, :] = ag[i, ROWS : 2 * ROWS, :]
    for which in (19, 23, 24, 25):
        wait_bytes(ag_in.at[0], recv.at[which])
    for i in range(CHIPS):
        rows = pl.ds(pl.multiple_of(other * HALF + i * ROWS, ROWS), ROWS)
        next_out[rows, :] = ag_in[i, 0:ROWS, :]
        next_ret[rows, :] = ag_in[i, ROWS : 2 * ROWS, :]

    wait_bytes(ids_all.at[pl.ds(0, NS - 1)], send.at[0])

    @pl.when(s < NS - 1)
    def _():
        wait_bytes(coef.at[here], send.at[1])
        wait_bytes(cot.at[here], send.at[27])

    @pl.when(s > 0)
    def _():
        wait_bytes(cot.at[here], send.at[2])
        wait_bytes(coef.at[here], send.at[26])

    wait_bytes(pieces.at[0, 0, 0], send.at[3])
    wait_bytes(w_all.at[:, pl.ds(0, (CHIPS - 1) * HD)], send.at[4])
    wait_bytes(gv_all.at[:, pl.ds(0, (CHIPS - 1) * HD)], send.at[5])
    wait_bytes(emb_in.at[pl.ds(0, NS - 1)], send.at[6])
    wait_bytes(v_in.at[pl.ds(0, CHIPS - 1)], send.at[7])
    wait_bytes(st_in.at[pl.ds(0, NT - 1)], send.at[8])
    wait_bytes(rs_in.at[pl.ds(0, CHIPS - 1)], send.at[9])
    wait_bytes(gg_in.at[pl.ds(0, NT - 1)], send.at[10])
    wait_bytes(pieces.at[0, pl.ds(0, NZ - 1)], send.at[11])
    wait_bytes(pieces.at[pl.ds(0, NX - 1)], send.at[12])
    wait_bytes(basis.at[0], send.at[13])
    wait_bytes(res.at[0], send.at[14])
    wait_bytes(gn_in, send.at[15])
    wait_bytes(in_in.at[pl.ds(0, CHIPS - 1)], send.at[16])
    wait_bytes(att_in, send.at[17])
    wait_bytes(write.at[0], send.at[18])
    for which in (19, 20, 21, 22, 23, 24, 25):
        wait_bytes(ag_in.at[0], send.at[which])


def shards(
    outgoing, returning, token_ids, shared_basis, embed_table, norm_gain, value_weight, write_basis, head_logits
):
    vmem = pl.BlockSpec(memory_space=pltpu.VMEM)
    hbm = pl.BlockSpec(memory_space=pl.ANY)
    next_out, next_ret, grad_write, grad_gain = pl.pallas_call(
        kernel,
        out_shape=(
            jax.ShapeDtypeStruct((TOK, R), BF16),
            jax.ShapeDtypeStruct((TOK, R), BF16),
            jax.ShapeDtypeStruct((HD, R), F32),
            jax.ShapeDtypeStruct((1, D), BF16),
        ),
        in_specs=[hbm] * 9,
        out_specs=(vmem, vmem, vmem, vmem),
        scratch_shapes=[
            pltpu.VMEM((8, WIDTH), BF16),
            pltpu.VMEM((FEAT, VOCAB), BF16),
            pltpu.VMEM((1, CHIP_W), F32),
            pltpu.VMEM((2, HD, R), BF16),
            pltpu.VMEM((TOK, TOK), BF16),
            pltpu.VMEM((2, 128), jnp.int32),
            pltpu.VMEM((4, 128), jnp.int32),
            pltpu.VMEM((NS, 4, 128), jnp.int32),
            pltpu.SMEM((NS, 4, 128), jnp.int32),
            pltpu.VMEM((TOK, R), BF16),
            pltpu.VMEM((TOK, R), BF16),
            pltpu.VMEM((NX, NZ, 2, 16, WIDTH // 2), BF16),
            pltpu.VMEM((2, R, WIDTH), BF16),
            pltpu.VMEM((CHIP_W, CHIPS * HD), BF16),
            pltpu.VMEM((VOCAB // 8, 128), F32),
            pltpu.VMEM((128, 128), F32),
            pltpu.VMEM((NS, 32, 128), BF16),
            pltpu.VMEM((NS, 32, 128), BF16),
            pltpu.VMEM((TOK, HD), BF16),
            pltpu.VMEM((TOK, CHIPS * HD), BF16),
            pltpu.VMEM((TOK, TOK), BF16),
            pltpu.VMEM((TOK, CHIP_W), F32),
            pltpu.VMEM((HALF, CHIP_W), F32),
            pltpu.VMEM((TOK, WIDTH), F32),
            pltpu.VMEM((2, TOK, WIDTH), BF16),
            pltpu.VMEM((TOK, CHIP_W), BF16),
            pltpu.VMEM((TOK, 128), F32),
            pltpu.VMEM((CHIPS, TOK, HD), BF16),
            pltpu.VMEM((CHIPS, TOK, HD), BF16),
            pltpu.VMEM((8, TOK), F32),
            pltpu.VMEM((NT, 8, TOK), F32),
            pltpu.VMEM((8, HALF), F32),
            pltpu.VMEM((CHIPS, 8, HALF), F32),
            pltpu.VMEM((2, HALF, WIDTH), BF16),
            pltpu.VMEM((2, HALF, WIDTH), BF16),
            pltpu.VMEM((TOK, HD), BF16),
            pltpu.VMEM((HALF, HD), BF16),
            pltpu.VMEM((CHIPS, 2 * ROWS, R), BF16),
            pltpu.VMEM((CHIPS, 2 * ROWS, R), BF16),
            pltpu.VMEM((CHIPS, 2 * ROWS, R), BF16),
            pltpu.VMEM((CHIPS, 2 * ROWS, R), BF16),
            pltpu.VMEM((16, 128), F32),
            pltpu.VMEM((NT, 16, 128), F32),
            pltpu.SemaphoreType.DMA((28,)),
            pltpu.SemaphoreType.DMA((28,)),
            pltpu.SemaphoreType.DMA((7,)),
        ],
        compiler_params=pltpu.CompilerParams(
            collective_id=0, has_side_effects=True, vmem_limit_bytes=52 * 2**20
        ),
        name="relay",
    )(
        outgoing, returning, token_ids.reshape(2, 128), shared_basis, embed_table, norm_gain, value_weight,
        write_basis, head_logits,
    )
    return (next_out, next_ret, grad_write[None], grad_gain)


def solution(mesh):
    placed = (
        P("section", None),
        P("section", None),
        P("section"),
        P("section", None),
        P(("tensor", "section"), None),
        P("section", None),
        P("section", None, "tensor"),
        P("section", "tensor", None),
        P("section", "tensor", None, None),
    )
    return jax.shard_map(
        shards,
        mesh=mesh,
        in_specs=placed,
        out_specs=(
            P("section", None),
            P("section", None),
            P("section", "tensor", None),
            P("section", None),
        ),
        check_vma=False,
    )
```

```python
import functools

import jax
import jax.numpy as jnp
from jax import lax
from jax.experimental import pallas as pl
from jax.experimental.pallas import tpu as pltpu
from jax.sharding import PartitionSpec as P

D = 8192
HD = 128
R = 512
TOK = 256
VOCAB = 65536
FEAT = 16
NS = 64
NT = 8
WIDTH = FEAT * NS
ROWS = TOK // NT
HALF = TOK // 2
CHIPS = 4
CHIP_W = 2 * WIDTH
NX = 4
NZ = 8
SIDE = NX * NZ
AT_X = 10
AT_ROWS = 44
AT_GRAD = 52
MESH = pl.DeviceIdType.MESH
F32 = jnp.float32
BF16 = jnp.bfloat16


def dot(a, b):
    return jnp.dot(a, b, preferred_element_type=F32)


def dot_nt(a, b):
    return lax.dot_general(a, b, (((1,), (1,)), ((), ())), preferred_element_type=F32)


def wait_bytes(view, sem):
    pltpu.make_async_copy(view, view, sem).wait()


def kernel(
    outgoing, returning, ids, basis_hbm, table_hbm, gain_hbm, weight, write_hbm, logits_hbm,
    next_out, next_ret, grad_write, grad_gain,
    basis_own, table, gain, write, logits,
    ids_raw, ids_all, ids_scalar, coef, cot, pieces, basis, w_all, table_t, stage,
    emb_out, emb_in, gv_own, gv_all, heads, gn, gn_in, res_c, res, ng, acc, v_out, v_in, st_out, st_in,
    in_out, in_in, g_hi, g_lo, att_own, att_in, rs_out, rs_in, rg_out, rg_in, ag, ag_in, ad, ad_in, gg_own, gg_in,
    send, recv, local,
):
    s = lax.axis_index("section")
    t = lax.axis_index("tensor")
    chip = t // 2
    core = lax.rem(t, 2)
    other = 1 - core
    y_lo = s // SIDE
    place = lax.rem(s, SIDE)
    z = lax.rem(s // NX, NZ)
    x = lax.rem(s, NX)

    def section_peer(k):
        return lax.rem(s + k, NS)

    def tensor_peer(k):
        return lax.rem(t + k, NT)

    def chip_peer(k):
        return lax.rem(chip + k, CHIPS)

    def fetch(src, dst, which):
        copy = pltpu.make_async_copy(src, dst, local.at[which])
        copy.start()
        return copy

    ids_copy = fetch(ids, ids_raw, 0)
    basis_copy = fetch(basis_hbm.at[:, pl.ds(pl.multiple_of(t * WIDTH, WIDTH), WIDTH)], basis_own, 1)
    table_copy = fetch(table_hbm, table, 2)
    logits_copy = fetch(logits_hbm.at[0, 0], logits, 3)
    write_copy = fetch(write_hbm.at[0], write.at[core], 4)
    gain_copy = fetch(gain_hbm.at[:, pl.ds(pl.multiple_of(chip * CHIP_W, CHIP_W), CHIP_W)], gain, 5)
    chip_rows = pl.ds(pl.multiple_of(chip * CHIP_W, CHIP_W), CHIP_W)
    own_cols = pl.ds(pl.multiple_of(chip * HD, HD), HD)
    w_copy = fetch(weight.at[0, chip_rows], w_all.at[:, own_cols], 6)

    barrier = pltpu.get_barrier_semaphore()

    def greet_section(k, c):
        pl.semaphore_signal(barrier, inc=1, device_id=(section_peer(k), t), device_id_type=MESH)
        return c

    def greet_tensor(k, c):
        pl.semaphore_signal(barrier, inc=1, device_id=(s, tensor_peer(k)), device_id_type=MESH)
        return c

    lax.fori_loop(1, NS, greet_section, 0)
    lax.fori_loop(1, NT, greet_tensor, 0)

    ids_copy.wait()
    own = ids_raw[...]
    ids_all[place, y_lo, 0:2, :] = (own >> 10) * 128 + (own & 127)
    ids_all[place, y_lo, 2:4, :] = (own >> 7) & 7
    basis_copy.wait()
    part = basis_own[...].astype(F32)
    pieces[x, z, y_lo] = jnp.concatenate([part[:, : WIDTH // 2], part[:, WIDTH // 2 :]], axis=0).astype(BF16)
    pl.semaphore_wait(barrier, NS + NT - 2)

    def push(src, dst, which, peer):
        pltpu.make_async_remote_copy(
            src_ref=src, dst_ref=dst, send_sem=send.at[which], recv_sem=recv.at[which],
            device_id=peer, device_id_type=MESH,
        ).start()

    def across(k):
        return (s, chip_peer(k) * 2 + core)

    partner = (s, chip * 2 + other)

    here = pl.ds(pl.multiple_of(core * HALF, HALF), HALF)
    there = pl.ds(pl.multiple_of(other * HALF, HALF), HALF)

    facing = (lax.rem(s + SIDE, NS), t)
    push(ids_all.at[place, y_lo], ids_all.at[place, y_lo], 19, facing)
    push(pieces.at[x, z, y_lo], pieces.at[x, z, y_lo], 3, facing)

    @pl.when(s > 0)
    def _():
        push(returning.at[here], cot.at[here], 2, (section_peer(NS - 1), t))

    @pl.when(s < NS - 1)
    def _():
        push(outgoing.at[here], coef.at[here], 1, (section_peer(1), t))


    wait_bytes(ids_all.at[0, 0], recv.at[19])

    def send_ids(k, c):
        push(ids_all.at[place], ids_all.at[place], 0, (y_lo * SIDE + lax.rem(place + k, SIDE), t))
        return c

    lax.fori_loop(1, SIDE, send_ids, 0)
    for k in (2, 1, 3):
        rows = pl.ds(pl.multiple_of(chip_peer(k) * CHIP_W, CHIP_W), CHIP_W)
        push(weight.at[0, rows], w_all.at[:, own_cols], 4, across(k))
    wait_bytes(pieces.at[0, 0, 0], recv.at[3])

    def send_z(k, c):
        push(pieces.at[x, z], pieces.at[x, z], 11, (y_lo * SIDE + lax.rem(z + k, NZ) * NX + x, t))
        return c

    lax.fori_loop(1, NZ, send_z, 0)
    write_copy.wait()
    push(write.at[core], write.at[core], 18, partner)

    table_copy.wait()

    def turn(b, c):
        tile = table[:, pl.ds(pl.multiple_of(b * 1024, 1024), 1024)]
        tile = jnp.concatenate([tile[:, v * 128 : (v + 1) * 128] for v in range(8)], axis=0)
        table_t[pl.ds(pl.multiple_of(b * 128, 128), 128), :] = tile.astype(F32).T
        return c

    lax.fori_loop(0, VOCAB // 1024, turn, 0)

    wait_bytes(ids_all.at[pl.ds(0, SIDE - 1)], recv.at[0])
    scalar_copy = fetch(ids_all, ids_scalar, 0)
    scalar_copy.wait()
    lane = lax.broadcasted_iota(jnp.int32, (8, 128), 1)
    sub = lax.broadcasted_iota(jnp.int32, (8, 128), 0)
    group = lane // FEAT

    def find(p, half):
        low = lax.rem(p, SIDE)
        high = p // SIDE
        groups = jnp.broadcast_to(ids_all[low, high, pl.ds(2 + half, 1), :], (8, 128))
        for j in range(128):
            stage[pl.ds(j, 1), :] = table_t[pl.ds(ids_scalar[low, high, half, j], 1), :]
        outs = []
        for q in range(2):
            place = jnp.take_along_axis(groups, 16 * group + 8 * q + sub, axis=1) * FEAT + lane % FEAT
            found = None
            for b in range(8):
                row = jnp.take_along_axis(stage[16 * b + 8 * q : 16 * b + 8 * q + 8, :], place, axis=1)
                found = row if found is None else jnp.where(group == b, row, found)
            outs.append(found)
        return jnp.concatenate(outs, axis=0).astype(BF16)

    def values_gradient():
        logits_copy.wait()
        query = lax.broadcasted_iota(jnp.int32, (TOK, TOK), 0)
        key = lax.broadcasted_iota(jnp.int32, (TOK, TOK), 1)
        scores = jnp.where(query >= key, logits[...].astype(F32), -1e30)
        expd = jnp.exp(scores - jnp.max(scores, axis=1, keepdims=True))
        soft = expd / jnp.sum(expd, axis=1, keepdims=True)
        heads[...] = soft.astype(BF16)
        to_turn = soft.T.astype(BF16)

        @pl.when(s < NS - 1)
        def _():
            wait_bytes(cot.at[here], recv.at[27])

        @pl.when(s == NS - 1)
        def _():
            last = pltpu.make_async_copy(returning, cot, local.at[0])
            last.start()
            last.wait()

        ga = dot_nt(cot[...], write[core]).astype(BF16)
        gv_own[...] = dot(to_turn, ga).astype(BF16)
        for j in (2, 1, 3):
            push(gv_own, gv_all.at[:, own_cols], 5, across(j))
        gv_all[:, own_cols] = gv_own[...]

    def look_up(k, c):
        p = section_peer(k)

        def one_half(half, cc):
            emb_out[p, pl.ds(pl.multiple_of(half * 16, 16), 16), :] = find(p, half)
            return cc

        lax.fori_loop(0, 2, one_half, 0)
        push(emb_out.at[p], emb_in.at[s], 6, (p, t))

        @pl.when(k == AT_X)
        def _():
            wait_bytes(pieces.at[0, pl.ds(0, NZ - 1)], recv.at[11])
            for j in (2, 1, 3):
                push(pieces.at[x], pieces.at[x], 12, (y_lo * SIDE + z * NX + lax.rem(x + j, NX), t))

        @pl.when(jnp.logical_and(k == AT_ROWS, s < NS - 1))
        def _():
            wait_bytes(cot.at[here], recv.at[2])
            push(cot.at[here], cot.at[here], 27, partner)

        @pl.when(jnp.logical_and(k == AT_ROWS, s > 0))
        def _():
            wait_bytes(coef.at[here], recv.at[1])
            push(coef.at[here], coef.at[here], 26, partner)

        @pl.when(k == AT_GRAD)
        def _():
            values_gradient()

        return c

    lax.fori_loop(1, NS, look_up, 0)

    def own_half(half, c):
        emb_in[s, pl.ds(pl.multiple_of(half * 16, 16), 16), :] = find(s, half)
        return c

    lax.fori_loop(0, 2, own_half, 0)

    wait_bytes(pieces.at[pl.ds(0, NX - 1)], recv.at[12])
    for lo in range(2):
        for zz in range(NZ):
            tile = pieces[:, zz, lo].astype(F32)
            for xx in range(NX):
                rows = slice((lo * NZ * NX + zz * NX + xx) * 8, (lo * NZ * NX + zz * NX + xx) * 8 + 8)
                if xx % 2 == 0:
                    pair = slice(rows.start, rows.start + 16)
                    for h in range(2):
                        both = jnp.concatenate([tile[xx, 8 * h : 8 * h + 8], tile[xx + 1, 8 * h : 8 * h + 8]], axis=0)
                        basis[core, pair, h * 512 : (h + 1) * 512] = both.astype(BF16)
    push(basis.at[core], basis.at[core], 13, partner)

    @pl.when(s > 0)
    def _():
        wait_bytes(coef.at[here], recv.at[26])

    @pl.when(s == 0)
    def _():
        coef[...] = jnp.zeros_like(coef)

    res_c[...] = dot(coef[...], basis[core])

    wait_bytes(emb_in.at[pl.ds(0, NS - 1)], recv.at[6])
    acc[...] = jnp.zeros_like(acc)
    lane16 = lax.broadcasted_iota(jnp.int32, (16, 128), 1) // FEAT

    def assemble(u, c):
        cols = pl.ds(pl.multiple_of(u * 128, 128), 128)
        for half in range(2):
            xs = [emb_in[8 * u + v, 16 * half : 16 * half + 16, :].astype(F32) for v in range(8)]
            for d in (4, 2, 1):
                low = (lane16 & d) == 0
                ys = list(xs)
                for v in range(8):
                    if v & d == 0:
                        a, b = xs[v], xs[v + d]
                        ys[v] = jnp.where(low, a, pltpu.roll(b, 16 * d, 1))
                        ys[v + d] = jnp.where(low, pltpu.roll(a, 128 - 16 * d, 1), b)
                xs = ys
            for b in range(8):
                rows = slice(128 * half + 16 * b, 128 * half + 16 * b + 16)
                r = (res_c[rows, cols] + xs[b]).astype(BF16)
                res[core, rows, cols] = r
                r = r.astype(F32)
                acc[rows, :] += r * r
        return c

    lax.fori_loop(0, WIDTH // 128, assemble, 0)
    push(res.at[core], res.at[core], 14, partner)
    st_out[...] = jnp.zeros_like(st_out)
    st_out[0:1, :] = jnp.sum(acc[...].T, axis=0, keepdims=True)

    def send_squares(k, c):
        push(st_out, st_in.at[t], 8, (s, tensor_peer(k)))
        return c

    lax.fori_loop(1, NT, send_squares, 0)
    st_in[t] = st_out[...]
    wait_bytes(st_in.at[pl.ds(0, NT - 1)], recv.at[8])
    total = st_in[0]
    for i in range(1, NT):
        total = total + st_in[i]
    inv_row = 1.0 / jnp.sqrt(total[0:1, :] / D + 1e-5)
    acc[...] = jnp.broadcast_to(inv_row, (128, TOK)).T
    gain_copy.wait()
    wait_bytes(res.at[0], recv.at[14])
    for i in range(2):

        def normalise(u, c):
            cols = pl.ds(pl.multiple_of(u * 128, 128), 128)
            wide = pl.ds(pl.multiple_of(i * WIDTH + u * 128, 128), 128)
            ng[:, wide] = (res[i, :, cols].astype(F32) * acc[...] * gain[:, wide]).astype(BF16)
            return c

        lax.fori_loop(0, WIDTH // 128, normalise, 0)

    w_copy.wait()
    wait_bytes(w_all.at[:, pl.ds(0, (CHIPS - 1) * HD)], recv.at[4])
    for h in range(2):
        v = dot(ng[...], w_all[:, h * 256 : (h + 1) * 256]).astype(BF16)
        v_out[2 * h] = v[:, :HD]
        v_out[2 * h + 1] = v[:, HD:]
    for k in (2, 1, 3):
        push(v_out.at[chip_peer(k)], v_in.at[chip], 7, across(k))
    v_in[chip] = v_out[chip]

    wait_bytes(gv_all.at[:, pl.ds(0, (CHIPS - 1) * HD)], recv.at[5])
    gn[...] = dot_nt(gv_all[...], w_all[...])
    push(gn.at[there], gn_in, 15, partner)
    inner = jnp.zeros((TOK, 128), F32)
    for u in range(CHIP_W // 128):
        cols = slice(u * 128, (u + 1) * 128)
        narrow = slice(u % 8 * 128, (u % 8 + 1) * 128)
        inner = inner + gn[:, cols] * gain[:, cols] * res[u // 8, :, narrow].astype(F32)
    in_out[...] = jnp.broadcast_to(jnp.sum(inner.T, axis=0, keepdims=True), (8, TOK))

    def send_inner(k, c):
        push(in_out, in_in.at[t], 16, (s, tensor_peer(k)))
        return c

    lax.fori_loop(1, NT, send_inner, 0)
    in_in[t] = in_out[...]

    wait_bytes(gn_in, recv.at[15])
    inv = acc[here, :]
    for u in range(CHIP_W // 128):
        cols = slice(u * 128, (u + 1) * 128)
        narrow = slice(u % 8 * 128, (u % 8 + 1) * 128)
        n = (gn[here, cols] + gn_in[:, cols]) * inv
        gn_in[:, cols] = n * gain[:, cols]
        gg_own[u : u + 1, :] = jnp.sum(n * res[u // 8, here, narrow].astype(F32), axis=0, keepdims=True)

    wait_bytes(v_in.at[pl.ds(0, CHIPS - 1)], recv.at[7])
    v = v_in[0].astype(F32)
    for i in range(1, CHIPS):
        v = v + v_in[i].astype(F32)
    attended = dot(heads[...], v.astype(BF16))
    att_own[...] = attended.astype(BF16)
    push(att_own.at[there], att_in, 17, partner)

    wait_bytes(in_in.at[pl.ds(0, NT - 1)], recv.at[16])
    total = in_in[0]
    for i in range(1, NT):
        total = total + in_in[i]
    acc[...] = jnp.broadcast_to(total[0:1, :], (128, TOK)).T
    back = acc[here, :] * inv * inv * inv / D
    for u in range(CHIP_W // 128):
        cols = slice(u * 128, (u + 1) * 128)
        narrow = slice(u % 8 * 128, (u % 8 + 1) * 128)
        g = gn_in[:, cols] - res[u // 8, here, narrow].astype(F32) * back
        upper = g.astype(BF16)
        g_hi[u // 8, :, narrow] = upper
        g_lo[u // 8, :, narrow] = (g - upper.astype(F32)).astype(BF16)
    wait_bytes(basis.at[0], recv.at[13])
    grad = dot_nt(g_hi[0], basis[0]) + dot_nt(g_lo[0], basis[0])
    grad = grad + (dot_nt(g_hi[1], basis[1]) + dot_nt(g_lo[1], basis[1]))
    grad = grad.astype(BF16)
    for i in range(CHIPS):
        rg_out[i] = grad[i * ROWS : (i + 1) * ROWS, :]
    for k in (2, 1, 3):
        push(rg_out.at[chip_peer(k)], rg_in.at[chip], 29, across(k))
    rg_in[chip] = rg_out[chip]

    wait_bytes(write.at[0], recv.at[18])
    delta = dot(att_own[here, :], write[core])
    wait_bytes(att_in, recv.at[17])
    delta = (delta + dot(att_in[...], write[other])).astype(BF16)
    for i in range(CHIPS):
        rs_out[i] = delta[i * ROWS : (i + 1) * ROWS, :]
    for k in (2, 1, 3):
        push(rs_out.at[chip_peer(k)], rs_in.at[chip], 9, across(k))
    rs_in[chip] = rs_out[chip]

    def send_gain(k, c):
        push(gg_own, gg_in.at[t], 10, (s, tensor_peer(k)))
        return c

    lax.fori_loop(1, NT, send_gain, 0)
    gg_in[t] = gg_own[...]
    mine = pl.ds(pl.multiple_of(core * HALF + chip * ROWS, ROWS), ROWS)

    def add_up(parts, base, to_all, to_core, first):
        total = base[mine, :].astype(F32)
        for i in range(CHIPS):
            total = total + parts[i].astype(F32)
        to_all[chip] = total.astype(BF16)
        for k in (2, 1, 3):
            push(to_all.at[chip], to_all.at[chip], first + k, across(k))
        push(to_all.at[chip], to_core.at[chip], first, partner)

    def forward(to_all, to_core, first):
        for k in (1, 3, 2):
            wait_bytes(to_all.at[0], recv.at[first + k])
            come = chip_peer(CHIPS - k)
            push(to_all.at[come], to_core.at[come], first + 3 + k, partner)

    def collect(to_all, to_core, first, out):
        for i in range(CHIPS):
            out[pl.ds(pl.multiple_of(core * HALF + i * ROWS, ROWS), ROWS), :] = to_all[i]
        for which in (first, first + 4, first + 5, first + 6):
            wait_bytes(to_core.at[0], recv.at[which])
        for i in range(CHIPS):
            out[pl.ds(pl.multiple_of(other * HALF + i * ROWS, ROWS), ROWS), :] = to_core[i]

    wait_bytes(rg_in.at[pl.ds(0, CHIPS - 1)], recv.at[29])
    add_up(rg_in, cot, ag, ag_in, 30)
    wait_bytes(rs_in.at[pl.ds(0, CHIPS - 1)], recv.at[9])
    add_up(rs_in, coef, ad, ad_in, 37)
    grad_write[...] = dot(attended.T.astype(BF16), cot[...])
    forward(ag, ag_in, 30)
    wait_bytes(gg_in.at[pl.ds(0, NT - 1)], recv.at[10])
    grad_gain[...] = jnp.concatenate(
        [gg_in[2 * i, j : j + 1, :] + gg_in[2 * i + 1, j : j + 1, :] for i in range(CHIPS) for j in range(16)], axis=1
    ).astype(BF16)
    forward(ad, ad_in, 37)
    collect(ag, ag_in, 30, next_ret)
    collect(ad, ad_in, 37, next_out)

    wait_bytes(ids_all.at[pl.ds(0, SIDE - 1)], send.at[0])
    wait_bytes(ids_all.at[0, 0], send.at[19])

    @pl.when(s < NS - 1)
    def _():
        wait_bytes(coef.at[here], send.at[1])
        wait_bytes(cot.at[here], send.at[27])

    @pl.when(s > 0)
    def _():
        wait_bytes(cot.at[here], send.at[2])
        wait_bytes(coef.at[here], send.at[26])

    wait_bytes(pieces.at[0, 0, 0], send.at[3])
    wait_bytes(w_all.at[:, pl.ds(0, (CHIPS - 1) * HD)], send.at[4])
    wait_bytes(gv_all.at[:, pl.ds(0, (CHIPS - 1) * HD)], send.at[5])
    wait_bytes(emb_in.at[pl.ds(0, NS - 1)], send.at[6])
    wait_bytes(v_in.at[pl.ds(0, CHIPS - 1)], send.at[7])
    wait_bytes(st_in.at[pl.ds(0, NT - 1)], send.at[8])
    wait_bytes(rs_in.at[pl.ds(0, CHIPS - 1)], send.at[9])
    wait_bytes(gg_in.at[pl.ds(0, NT - 1)], send.at[10])
    wait_bytes(pieces.at[0, pl.ds(0, NZ - 1)], send.at[11])
    wait_bytes(pieces.at[pl.ds(0, NX - 1)], send.at[12])
    wait_bytes(basis.at[0], send.at[13])
    wait_bytes(res.at[0], send.at[14])
    wait_bytes(gn_in, send.at[15])
    wait_bytes(in_in.at[pl.ds(0, NT - 1)], send.at[16])
    wait_bytes(att_in, send.at[17])
    wait_bytes(write.at[0], send.at[18])
    wait_bytes(rg_in.at[pl.ds(0, CHIPS - 1)], send.at[29])
    for which in range(30, 44):
        wait_bytes(ag_in.at[0], send.at[which])


def shards(
    outgoing, returning, token_ids, shared_basis, embed_table, norm_gain, value_weight, write_basis, head_logits
):
    vmem = pl.BlockSpec(memory_space=pltpu.VMEM)
    hbm = pl.BlockSpec(memory_space=pl.ANY)
    next_out, next_ret, grad_write, grad_gain = pl.pallas_call(
        kernel,
        out_shape=(
            jax.ShapeDtypeStruct((TOK, R), BF16),
            jax.ShapeDtypeStruct((TOK, R), BF16),
            jax.ShapeDtypeStruct((HD, R), F32),
            jax.ShapeDtypeStruct((1, D), BF16),
        ),
        in_specs=[hbm] * 9,
        out_specs=(vmem, vmem, vmem, vmem),
        scratch_shapes=[
            pltpu.VMEM((8, WIDTH), BF16),
            pltpu.VMEM((FEAT, VOCAB), BF16),
            pltpu.VMEM((1, CHIP_W), F32),
            pltpu.VMEM((2, HD, R), BF16),
            pltpu.VMEM((TOK, TOK), BF16),
            pltpu.VMEM((2, 128), jnp.int32),
            pltpu.VMEM((SIDE, 2, 4, 128), jnp.int32),
            pltpu.SMEM((SIDE, 2, 4, 128), jnp.int32),
            pltpu.VMEM((TOK, R), BF16),
            pltpu.VMEM((TOK, R), BF16),
            pltpu.VMEM((NX, NZ, 2, 16, WIDTH // 2), BF16),
            pltpu.VMEM((2, R, WIDTH), BF16),
            pltpu.VMEM((CHIP_W, CHIPS * HD), BF16),
            pltpu.VMEM((VOCAB // 8, 128), F32),
            pltpu.VMEM((128, 128), F32),
            pltpu.VMEM((NS, 32, 128), BF16),
            pltpu.VMEM((NS, 32, 128), BF16),
            pltpu.VMEM((TOK, HD), BF16),
            pltpu.VMEM((TOK, CHIPS * HD), BF16),
            pltpu.VMEM((TOK, TOK), BF16),
            pltpu.VMEM((TOK, CHIP_W), F32),
            pltpu.VMEM((HALF, CHIP_W), F32),
            pltpu.VMEM((TOK, WIDTH), F32),
            pltpu.VMEM((2, TOK, WIDTH), BF16),
            pltpu.VMEM((TOK, CHIP_W), BF16),
            pltpu.VMEM((TOK, 128), F32),
            pltpu.VMEM((CHIPS, TOK, HD), BF16),
            pltpu.VMEM((CHIPS, TOK, HD), BF16),
            pltpu.VMEM((8, TOK), F32),
            pltpu.VMEM((NT, 8, TOK), F32),
            pltpu.VMEM((8, TOK), F32),
            pltpu.VMEM((NT, 8, TOK), F32),
            pltpu.VMEM((2, HALF, WIDTH), BF16),
            pltpu.VMEM((2, HALF, WIDTH), BF16),
            pltpu.VMEM((TOK, HD), BF16),
            pltpu.VMEM((HALF, HD), BF16),
            pltpu.VMEM((CHIPS, ROWS, R), BF16),
            pltpu.VMEM((CHIPS, ROWS, R), BF16),
            pltpu.VMEM((CHIPS, ROWS, R), BF16),
            pltpu.VMEM((CHIPS, ROWS, R), BF16),
            pltpu.VMEM((CHIPS, ROWS, R), BF16),
            pltpu.VMEM((CHIPS, ROWS, R), BF16),
            pltpu.VMEM((CHIPS, ROWS, R), BF16),
            pltpu.VMEM((CHIPS, ROWS, R), BF16),
            pltpu.VMEM((16, 128), F32),
            pltpu.VMEM((NT, 16, 128), F32),
            pltpu.SemaphoreType.DMA((44,)),
            pltpu.SemaphoreType.DMA((44,)),
            pltpu.SemaphoreType.DMA((7,)),
        ],
        compiler_params=pltpu.CompilerParams(
            collective_id=0, has_side_effects=True, vmem_limit_bytes=52 * 2**20
        ),
        name="relay",
    )(
        outgoing, returning, token_ids.reshape(2, 128), shared_basis, embed_table, norm_gain, value_weight,
        write_basis, head_logits,
    )
    return (next_out, next_ret, grad_write[None], grad_gain)


def solution(mesh):
    placed = (
        P("section", None),
        P("section", None),
        P("section"),
        P("section", None),
        P(("tensor", "section"), None),
        P("section", None),
        P("section", None, "tensor"),
        P("section", "tensor", None),
        P("section", "tensor", None, None),
    )
    return jax.shard_map(
        shards,
        mesh=mesh,
        in_specs=placed,
        out_specs=(
            P("section", None),
            P("section", None),
            P("section", "tensor", None),
            P("section", None),
        ),
        check_vma=False,
    )
```

```python
import functools

import jax
import jax.numpy as jnp
from jax import lax
from jax.experimental import pallas as pl
from jax.experimental.pallas import tpu as pltpu
from jax.sharding import PartitionSpec as P

D = 8192
HD = 128
R = 512
TOK = 256
VOCAB = 65536
FEAT = 16
NS = 64
NT = 8
WIDTH = FEAT * NS
ROWS = TOK // NT
HALF = TOK // 2
CHIPS = 4
CHIP_W = 2 * WIDTH
NX = 4
NZ = 8
SIDE = NX * NZ
AT_X = 10
TURN_FIRST = 14
AT_ROWS = 44
AT_GRAD = 52
MESH = pl.DeviceIdType.MESH
F32 = jnp.float32
BF16 = jnp.bfloat16


def dot(a, b):
    return jnp.dot(a, b, preferred_element_type=F32)


def dot_nt(a, b):
    return lax.dot_general(a, b, (((1,), (1,)), ((), ())), preferred_element_type=F32)


def wait_bytes(view, sem):
    pltpu.make_async_copy(view, view, sem).wait()


def kernel(
    outgoing, returning, ids, basis_hbm, table_hbm, gain_hbm, weight, write_hbm, logits_hbm,
    next_out, next_ret, grad_write, grad_gain,
    basis_own, table, gain, write, logits,
    ids_raw, ids_all, ids_scalar, coef, cot, pieces, basis, w_all, table_t, stage,
    emb_out, emb_in, gv_own, gv_all, heads, gn, gn_in, res_c, res, ng, acc, v_out, v_in, st_out, st_in,
    in_out, in_in, g_hi, g_lo, att_own, att_in, rs_out, rs_in, rg_out, rg_in, ag, ag_in, ad, ad_in, gg_own, gg_in, gg_all, gw,
    send, recv, local,
):
    s = lax.axis_index("section")
    t = lax.axis_index("tensor")
    chip = t // 2
    core = lax.rem(t, 2)
    other = 1 - core
    y_lo = s // SIDE
    place = lax.rem(s, SIDE)
    z = lax.rem(s // NX, NZ)
    x = lax.rem(s, NX)

    def section_peer(k):
        return lax.rem(s + k, NS)

    def tensor_peer(k):
        return lax.rem(t + k, NT)

    def chip_peer(k):
        return lax.rem(chip + k, CHIPS)

    def fetch(src, dst, which):
        copy = pltpu.make_async_copy(src, dst, local.at[which])
        copy.start()
        return copy

    ids_copy = fetch(ids, ids_raw, 0)
    basis_copy = fetch(basis_hbm.at[:, pl.ds(pl.multiple_of(t * WIDTH, WIDTH), WIDTH)], basis_own, 1)
    table_copy = fetch(table_hbm, table, 2)
    logits_copy = fetch(logits_hbm.at[0, 0], logits, 3)
    write_copy = fetch(write_hbm.at[0], write.at[core], 4)
    gain_copy = fetch(gain_hbm.at[:, pl.ds(pl.multiple_of(chip * CHIP_W, CHIP_W), CHIP_W)], gain, 5)
    chip_rows = pl.ds(pl.multiple_of(chip * CHIP_W, CHIP_W), CHIP_W)
    own_cols = pl.ds(pl.multiple_of(chip * HD, HD), HD)
    w_copy = fetch(weight.at[0, chip_rows], w_all.at[:, own_cols], 6)

    barrier = pltpu.get_barrier_semaphore()

    def greet_section(k, c):
        pl.semaphore_signal(barrier, inc=1, device_id=(section_peer(k), t), device_id_type=MESH)
        return c

    def greet_tensor(k, c):
        pl.semaphore_signal(barrier, inc=1, device_id=(s, tensor_peer(k)), device_id_type=MESH)
        return c

    lax.fori_loop(1, NS, greet_section, 0)
    lax.fori_loop(1, NT, greet_tensor, 0)

    ids_copy.wait()
    own = ids_raw[...]
    ids_all[place, y_lo, 0:2, :] = (own >> 10) * 128 + (own & 127)
    ids_all[place, y_lo, 2:4, :] = (own >> 7) & 7
    basis_copy.wait()
    part = basis_own[...].astype(F32)
    pieces[x, z, y_lo] = jnp.concatenate([part[:, : WIDTH // 2], part[:, WIDTH // 2 :]], axis=0).astype(BF16)
    pl.semaphore_wait(barrier, NS + NT - 2)

    def push(src, dst, which, peer):
        pltpu.make_async_remote_copy(
            src_ref=src, dst_ref=dst, send_sem=send.at[which], recv_sem=recv.at[which],
            device_id=peer, device_id_type=MESH,
        ).start()

    def across(k):
        return (s, chip_peer(k) * 2 + core)

    partner = (s, chip * 2 + other)

    here = pl.ds(pl.multiple_of(core * HALF, HALF), HALF)
    there = pl.ds(pl.multiple_of(other * HALF, HALF), HALF)

    facing = (lax.rem(s + SIDE, NS), t)
    push(ids_all.at[place, y_lo], ids_all.at[place, y_lo], 19, facing)
    push(pieces.at[x, z, y_lo], pieces.at[x, z, y_lo], 3, facing)

    @pl.when(s > 0)
    def _():
        push(returning.at[here], cot.at[here], 2, (section_peer(NS - 1), t))

    @pl.when(s < NS - 1)
    def _():
        push(outgoing.at[here], coef.at[here], 1, (section_peer(1), t))


    table_copy.wait()

    def turn(b, c):
        tile = table[:, pl.ds(pl.multiple_of(b * 1024, 1024), 1024)]
        tile = jnp.concatenate([tile[:, v * 128 : (v + 1) * 128] for v in range(8)], axis=0)
        table_t[pl.ds(pl.multiple_of(b * 128, 128), 128), :] = tile.T.astype(F32)
        return c

    lax.fori_loop(0, TURN_FIRST, turn, 0)
    wait_bytes(ids_all.at[0, 0], recv.at[19])

    def send_ids(k, c):
        push(ids_all.at[place], ids_all.at[place], 0, (y_lo * SIDE + lax.rem(place + k, SIDE), t))
        return c

    lax.fori_loop(1, SIDE, send_ids, 0)
    for k in (2, 1, 3):
        rows = pl.ds(pl.multiple_of(chip_peer(k) * CHIP_W, CHIP_W), CHIP_W)
        push(weight.at[0, rows], w_all.at[:, own_cols], 4, across(k))
    wait_bytes(pieces.at[0, 0, 0], recv.at[3])

    def send_z(k, c):
        push(pieces.at[x, z], pieces.at[x, z], 11, (y_lo * SIDE + lax.rem(z + k, NZ) * NX + x, t))
        return c

    lax.fori_loop(1, NZ, send_z, 0)
    write_copy.wait()
    push(write.at[core], write.at[core], 18, partner)
    lax.fori_loop(TURN_FIRST, VOCAB // 1024, turn, 0)

    wait_bytes(ids_all.at[pl.ds(0, SIDE - 1)], recv.at[0])
    scalar_copy = fetch(ids_all, ids_scalar, 0)
    scalar_copy.wait()
    lane = lax.broadcasted_iota(jnp.int32, (8, 128), 1)
    sub = lax.broadcasted_iota(jnp.int32, (8, 128), 0)
    group = lane // FEAT

    def find(p, half):
        low = lax.rem(p, SIDE)
        high = p // SIDE
        groups = jnp.broadcast_to(ids_all[low, high, pl.ds(2 + half, 1), :], (8, 128))
        for j in range(0, 128, 16):
            found = [table_t[pl.ds(ids_scalar[low, high, half, j + i], 1), :] for i in range(16)]
            for i in range(16):
                stage[pl.ds(j + i, 1), :] = found[i]
        outs = []
        for q in range(2):
            place = jnp.take_along_axis(groups, 16 * group + 8 * q + sub, axis=1) * FEAT + lane % FEAT
            found = None
            for b in range(8):
                row = jnp.take_along_axis(stage[16 * b + 8 * q : 16 * b + 8 * q + 8, :], place, axis=1)
                found = row if found is None else jnp.where(group == b, row, found)
            outs.append(found)
        return jnp.concatenate(outs, axis=0).astype(BF16)


    def values_gradient():
        logits_copy.wait()
        query = lax.broadcasted_iota(jnp.int32, (TOK, TOK), 0)
        key = lax.broadcasted_iota(jnp.int32, (TOK, TOK), 1)
        scores = jnp.where(query >= key, logits[...].astype(F32), -1e30)
        expd = jnp.exp(scores - jnp.max(scores, axis=1, keepdims=True))
        soft = expd / jnp.sum(expd, axis=1, keepdims=True)
        heads[...] = soft.astype(BF16)
        to_turn = soft.T.astype(BF16)

        @pl.when(s < NS - 1)
        def _():
            wait_bytes(cot.at[here], recv.at[27])

        @pl.when(s == NS - 1)
        def _():
            last = pltpu.make_async_copy(returning, cot, local.at[0])
            last.start()
            last.wait()

        ga = dot_nt(cot[...], write[core]).astype(BF16)
        gv_own[...] = dot(to_turn, ga).astype(BF16)
        for j in (2, 1, 3):
            push(gv_own, gv_all.at[:, own_cols], 5, across(j))
        gv_all[:, own_cols] = gv_own[...]

    def look_up(k, c):
        p = section_peer(k)

        def one_half(half, cc):
            emb_out[p, pl.ds(pl.multiple_of(half * 16, 16), 16), :] = find(p, half)
            return cc

        lax.fori_loop(0, 2, one_half, 0)
        push(emb_out.at[p], emb_in.at[s], 6, (p, t))

        @pl.when(k == AT_X)
        def _():
            wait_bytes(pieces.at[0, pl.ds(0, NZ - 1)], recv.at[11])
            for j in (2, 1, 3):
                push(pieces.at[x], pieces.at[x], 12, (y_lo * SIDE + z * NX + lax.rem(x + j, NX), t))

        @pl.when(jnp.logical_and(k == AT_ROWS, s < NS - 1))
        def _():
            wait_bytes(cot.at[here], recv.at[2])
            push(cot.at[here], cot.at[here], 27, partner)

        @pl.when(jnp.logical_and(k == AT_ROWS, s > 0))
        def _():
            wait_bytes(coef.at[here], recv.at[1])
            push(coef.at[here], coef.at[here], 26, partner)

        @pl.when(k == AT_GRAD)
        def _():
            values_gradient()

        return c

    lax.fori_loop(1, NS, look_up, 0)

    def own_half(half, c):
        emb_in[s, pl.ds(pl.multiple_of(half * 16, 16), 16), :] = find(s, half)
        return c

    lax.fori_loop(0, 2, own_half, 0)

    wait_bytes(pieces.at[pl.ds(0, NX - 1)], recv.at[12])
    for lo in range(2):
        for zz in range(NZ):
            tile = pieces[:, zz, lo].astype(F32)
            for xx in range(NX):
                rows = slice((lo * NZ * NX + zz * NX + xx) * 8, (lo * NZ * NX + zz * NX + xx) * 8 + 8)
                if xx % 2 == 0:
                    pair = slice(rows.start, rows.start + 16)
                    for h in range(2):
                        both = jnp.concatenate([tile[xx, 8 * h : 8 * h + 8], tile[xx + 1, 8 * h : 8 * h + 8]], axis=0)
                        basis[core, pair, h * 512 : (h + 1) * 512] = both.astype(BF16)
    push(basis.at[core], basis.at[core], 13, partner)

    @pl.when(s > 0)
    def _():
        wait_bytes(coef.at[here], recv.at[26])

    @pl.when(s == 0)
    def _():
        coef[...] = jnp.zeros_like(coef)

    res_c[...] = dot(coef[...], basis[core])

    wait_bytes(emb_in.at[pl.ds(0, NS - 1)], recv.at[6])
    acc[...] = jnp.zeros_like(acc)
    lane16 = lax.broadcasted_iota(jnp.int32, (16, 128), 1) // FEAT

    def assemble(u, c):
        cols = pl.ds(pl.multiple_of(u * 128, 128), 128)
        for half in range(2):
            xs = [emb_in[8 * u + v, 16 * half : 16 * half + 16, :].astype(F32) for v in range(8)]
            for d in (4, 2, 1):
                low = (lane16 & d) == 0
                ys = list(xs)
                for v in range(8):
                    if v & d == 0:
                        a, b = xs[v], xs[v + d]
                        ys[v] = jnp.where(low, a, pltpu.roll(b, 16 * d, 1))
                        ys[v + d] = jnp.where(low, pltpu.roll(a, 128 - 16 * d, 1), b)
                xs = ys
            for b in range(8):
                rows = slice(128 * half + 16 * b, 128 * half + 16 * b + 16)
                r = (res_c[rows, cols] + xs[b]).astype(BF16)
                res[core, rows, cols] = r
                r = r.astype(F32)
                acc[rows, :] += r * r
        return c

    lax.fori_loop(0, WIDTH // 128, assemble, 0)
    push(res.at[core], res.at[core], 14, partner)
    st_out[...] = jnp.zeros_like(st_out)
    st_out[0:1, :] = jnp.sum(acc[...].T, axis=0, keepdims=True)

    def send_squares(k, c):
        push(st_out, st_in.at[t], 8, (s, tensor_peer(k)))
        return c

    lax.fori_loop(1, NT, send_squares, 0)
    st_in[t] = st_out[...]
    wait_bytes(st_in.at[pl.ds(0, NT - 1)], recv.at[8])
    total = st_in[0]
    for i in range(1, NT):
        total = total + st_in[i]
    inv_row = 1.0 / jnp.sqrt(total[0:1, :] / D + 1e-5)
    acc[...] = jnp.broadcast_to(inv_row, (128, TOK)).T
    gain_copy.wait()
    wait_bytes(res.at[0], recv.at[14])
    for i in range(2):

        def normalise(u, c):
            cols = pl.ds(pl.multiple_of(u * 128, 128), 128)
            wide = pl.ds(pl.multiple_of(i * WIDTH + u * 128, 128), 128)
            ng[:, wide] = (res[i, :, cols].astype(F32) * acc[...] * gain[:, wide]).astype(BF16)
            return c

        lax.fori_loop(0, WIDTH // 128, normalise, 0)

    w_copy.wait()
    wait_bytes(w_all.at[:, pl.ds(0, (CHIPS - 1) * HD)], recv.at[4])
    wait_bytes(gv_all.at[:, pl.ds(0, (CHIPS - 1) * HD)], recv.at[5])
    gn[...] = dot_nt(gv_all[...], w_all[...])
    push(gn.at[there], gn_in, 15, partner)
    inner = jnp.zeros((TOK, 128), F32)
    for u in range(CHIP_W // 128):
        cols = slice(u * 128, (u + 1) * 128)
        narrow = slice(u % 8 * 128, (u % 8 + 1) * 128)
        inner = inner + gn[:, cols] * gain[:, cols] * res[u // 8, :, narrow].astype(F32)
    in_out[...] = jnp.broadcast_to(jnp.sum(inner.T, axis=0, keepdims=True), (8, TOK))

    def send_inner(k, c):
        push(in_out, in_in.at[t], 16, (s, tensor_peer(k)))
        return c

    lax.fori_loop(1, NT, send_inner, 0)
    in_in[t] = in_out[...]

    for h in range(2):
        v = dot(ng[...], w_all[:, h * 256 : (h + 1) * 256]).astype(BF16)
        v_out[2 * h] = v[:, :HD]
        v_out[2 * h + 1] = v[:, HD:]
    for k in (2, 1, 3):
        push(v_out.at[chip_peer(k)], v_in.at[chip], 7, across(k))
    v_in[chip] = v_out[chip]

    wait_bytes(gn_in, recv.at[15])
    inv = acc[here, :]
    for u in range(CHIP_W // 128):
        cols = slice(u * 128, (u + 1) * 128)
        narrow = slice(u % 8 * 128, (u % 8 + 1) * 128)
        n = (gn[here, cols] + gn_in[:, cols]) * inv
        gn_in[:, cols] = n * gain[:, cols]
        gg_own[u : u + 1, :] = jnp.sum(n * res[u // 8, here, narrow].astype(F32), axis=0, keepdims=True)

    wait_bytes(v_in.at[pl.ds(0, CHIPS - 1)], recv.at[7])
    v = v_in[0].astype(F32)
    for i in range(1, CHIPS):
        v = v + v_in[i].astype(F32)
    attended = dot(heads[...], v.astype(BF16))
    att_own[...] = attended.astype(BF16)
    push(att_own.at[there], att_in, 17, partner)

    wait_bytes(in_in.at[pl.ds(0, NT - 1)], recv.at[16])
    total = in_in[0]
    for i in range(1, NT):
        total = total + in_in[i]
    acc[...] = jnp.broadcast_to(total[0:1, :], (128, TOK)).T
    back = acc[here, :] * inv * inv * inv / D
    for u in range(CHIP_W // 128):
        cols = slice(u * 128, (u + 1) * 128)
        narrow = slice(u % 8 * 128, (u % 8 + 1) * 128)
        g = gn_in[:, cols] - res[u // 8, here, narrow].astype(F32) * back
        upper = g.astype(BF16)
        g_hi[u // 8, :, narrow] = upper
        g_lo[u // 8, :, narrow] = (g - upper.astype(F32)).astype(BF16)
    wait_bytes(basis.at[0], recv.at[13])
    grad = dot_nt(g_hi[0], basis[0]) + dot_nt(g_lo[0], basis[0])
    grad = grad + (dot_nt(g_hi[1], basis[1]) + dot_nt(g_lo[1], basis[1]))
    grad = grad.astype(BF16)
    for i in range(CHIPS):
        rg_out[i] = grad[i * ROWS : (i + 1) * ROWS, :]
    for k in (2, 1, 3):
        push(rg_out.at[chip_peer(k)], rg_in.at[chip], 29, across(k))
    rg_in[chip] = rg_out[chip]

    wait_bytes(write.at[0], recv.at[18])
    delta = dot(att_own[here, :], write[core])
    wait_bytes(att_in, recv.at[17])
    delta = (delta + dot(att_in[...], write[other])).astype(BF16)
    for i in range(CHIPS):
        rs_out[i] = delta[i * ROWS : (i + 1) * ROWS, :]
    for k in (2, 1, 3):
        push(rs_out.at[chip_peer(k)], rs_in.at[chip], 9, across(k))
    rs_in[chip] = rs_out[chip]

    def send_gain(k, c):
        push(gg_own, gg_in.at[t], 10, (s, tensor_peer(k)))
        return c

    lax.fori_loop(1, NT, send_gain, 0)
    gg_in[t] = gg_own[...]
    mine = pl.ds(pl.multiple_of(core * HALF + chip * ROWS, ROWS), ROWS)

    def add_up(parts, base, to_all, to_core, first):
        total = base[mine, :].astype(F32)
        for i in range(CHIPS):
            total = total + parts[i].astype(F32)
        to_all[chip] = total.astype(BF16)
        for k in (2, 1, 3):
            push(to_all.at[chip], to_all.at[chip], first + k, across(k))
        push(to_all.at[chip], to_core.at[chip], first, partner)

    def forward(to_all, to_core, first):
        for k in (1, 3, 2):
            wait_bytes(to_all.at[0], recv.at[first + k])
            come = chip_peer(CHIPS - k)
            push(to_all.at[come], to_core.at[come], first + 3 + k, partner)

    def put(parts, whose, out, which):
        for i in range(CHIPS):
            rows = pl.ds(pl.multiple_of(whose * HALF + i * ROWS, ROWS), ROWS)
            pltpu.make_async_copy(parts.at[i], out.at[rows], local.at[which]).start()

    def collect(to_all, to_core, first, out, which):
        put(to_all, core, out, which)
        for k in (first, first + 4, first + 5, first + 6):
            wait_bytes(to_core.at[0], recv.at[k])
        put(to_core, other, out, which)

    wait_bytes(rg_in.at[pl.ds(0, CHIPS - 1)], recv.at[29])
    add_up(rg_in, cot, ag, ag_in, 30)
    wait_bytes(rs_in.at[pl.ds(0, CHIPS - 1)], recv.at[9])
    add_up(rs_in, coef, ad, ad_in, 37)
    gw[...] = dot(attended.T.astype(BF16), cot[...])
    gw_copy = fetch(gw, grad_write, 3)
    forward(ag, ag_in, 30)
    wait_bytes(gg_in.at[pl.ds(0, NT - 1)], recv.at[10])
    gg_all[...] = jnp.concatenate(
        [gg_in[2 * i, j : j + 1, :] + gg_in[2 * i + 1, j : j + 1, :] for i in range(CHIPS) for j in range(16)], axis=1
    ).astype(BF16)
    gg_copy = fetch(gg_all, grad_gain, 4)
    forward(ad, ad_in, 37)
    collect(ag, ag_in, 30, next_ret, 1)
    collect(ad, ad_in, 37, next_out, 2)
    wait_bytes(next_ret, local.at[1])
    wait_bytes(next_out, local.at[2])
    gw_copy.wait()
    gg_copy.wait()

    wait_bytes(ids_all.at[pl.ds(0, SIDE - 1)], send.at[0])
    wait_bytes(ids_all.at[0, 0], send.at[19])

    @pl.when(s < NS - 1)
    def _():
        wait_bytes(coef.at[here], send.at[1])
        wait_bytes(cot.at[here], send.at[27])

    @pl.when(s > 0)
    def _():
        wait_bytes(cot.at[here], send.at[2])
        wait_bytes(coef.at[here], send.at[26])

    wait_bytes(pieces.at[0, 0, 0], send.at[3])
    wait_bytes(w_all.at[:, pl.ds(0, (CHIPS - 1) * HD)], send.at[4])
    wait_bytes(gv_all.at[:, pl.ds(0, (CHIPS - 1) * HD)], send.at[5])
    wait_bytes(emb_in.at[pl.ds(0, NS - 1)], send.at[6])
    wait_bytes(v_in.at[pl.ds(0, CHIPS - 1)], send.at[7])
    wait_bytes(st_in.at[pl.ds(0, NT - 1)], send.at[8])
    wait_bytes(rs_in.at[pl.ds(0, CHIPS - 1)], send.at[9])
    wait_bytes(gg_in.at[pl.ds(0, NT - 1)], send.at[10])
    wait_bytes(pieces.at[0, pl.ds(0, NZ - 1)], send.at[11])
    wait_bytes(pieces.at[pl.ds(0, NX - 1)], send.at[12])
    wait_bytes(basis.at[0], send.at[13])
    wait_bytes(res.at[0], send.at[14])
    wait_bytes(gn_in, send.at[15])
    wait_bytes(in_in.at[pl.ds(0, NT - 1)], send.at[16])
    wait_bytes(att_in, send.at[17])
    wait_bytes(write.at[0], send.at[18])
    wait_bytes(rg_in.at[pl.ds(0, CHIPS - 1)], send.at[29])
    for which in range(30, 44):
        wait_bytes(ag_in.at[0], send.at[which])


def hand_over(a, b, c, d, a_out, b_out, c_out, d_out, a_here, b_here, c_here, d_here, sem):
    steps = ((a, a_here, a_out), (b, b_here, b_out), (c, c_here, c_out), (d, d_here, d_out))
    into = [pltpu.make_async_copy(src, here, sem.at[i]) for i, (src, here, _) in enumerate(steps)]
    out = [pltpu.make_async_copy(here, dst, sem.at[4 + i]) for i, (_, here, dst) in enumerate(steps)]
    for copy in into:
        copy.start()
    for first, second in zip(into, out):
        first.wait()
        second.start()
    for copy in out:
        copy.wait()


def shards(
    outgoing, returning, token_ids, shared_basis, embed_table, norm_gain, value_weight, write_basis, head_logits
):
    hbm = pl.BlockSpec(memory_space=pl.ANY)
    results = (
        jax.ShapeDtypeStruct((TOK, R), BF16),
        jax.ShapeDtypeStruct((TOK, R), BF16),
        jax.ShapeDtypeStruct((HD, R), F32),
        jax.ShapeDtypeStruct((1, D), BF16),
    )
    made = pl.pallas_call(
        kernel,
        out_shape=results,
        in_specs=[hbm] * 9,
        out_specs=(hbm,) * 4,
        scratch_shapes=[
            pltpu.VMEM((8, WIDTH), BF16),
            pltpu.VMEM((FEAT, VOCAB), BF16),
            pltpu.VMEM((1, CHIP_W), F32),
            pltpu.VMEM((2, HD, R), BF16),
            pltpu.VMEM((TOK, TOK), BF16),
            pltpu.VMEM((2, 128), jnp.int32),
            pltpu.VMEM((SIDE, 2, 4, 128), jnp.int32),
            pltpu.SMEM((SIDE, 2, 4, 128), jnp.int32),
            pltpu.VMEM((TOK, R), BF16),
            pltpu.VMEM((TOK, R), BF16),
            pltpu.VMEM((NX, NZ, 2, 16, WIDTH // 2), BF16),
            pltpu.VMEM((2, R, WIDTH), BF16),
            pltpu.VMEM((CHIP_W, CHIPS * HD), BF16),
            pltpu.VMEM((VOCAB // 8, 128), F32),
            pltpu.VMEM((128, 128), F32),
            pltpu.VMEM((NS, 32, 128), BF16),
            pltpu.VMEM((NS, 32, 128), BF16),
            pltpu.VMEM((TOK, HD), BF16),
            pltpu.VMEM((TOK, CHIPS * HD), BF16),
            pltpu.VMEM((TOK, TOK), BF16),
            pltpu.VMEM((TOK, CHIP_W), F32),
            pltpu.VMEM((HALF, CHIP_W), F32),
            pltpu.VMEM((TOK, WIDTH), F32),
            pltpu.VMEM((2, TOK, WIDTH), BF16),
            pltpu.VMEM((TOK, CHIP_W), BF16),
            pltpu.VMEM((TOK, 128), F32),
            pltpu.VMEM((CHIPS, TOK, HD), BF16),
            pltpu.VMEM((CHIPS, TOK, HD), BF16),
            pltpu.VMEM((8, TOK), F32),
            pltpu.VMEM((NT, 8, TOK), F32),
            pltpu.VMEM((8, TOK), F32),
            pltpu.VMEM((NT, 8, TOK), F32),
            pltpu.VMEM((2, HALF, WIDTH), BF16),
            pltpu.VMEM((2, HALF, WIDTH), BF16),
            pltpu.VMEM((TOK, HD), BF16),
            pltpu.VMEM((HALF, HD), BF16),
            pltpu.VMEM((CHIPS, ROWS, R), BF16),
            pltpu.VMEM((CHIPS, ROWS, R), BF16),
            pltpu.VMEM((CHIPS, ROWS, R), BF16),
            pltpu.VMEM((CHIPS, ROWS, R), BF16),
            pltpu.VMEM((CHIPS, ROWS, R), BF16),
            pltpu.VMEM((CHIPS, ROWS, R), BF16),
            pltpu.VMEM((CHIPS, ROWS, R), BF16),
            pltpu.VMEM((CHIPS, ROWS, R), BF16),
            pltpu.VMEM((16, 128), F32),
            pltpu.VMEM((NT, 16, 128), F32),
            pltpu.VMEM((1, D), BF16),
            pltpu.VMEM((HD, R), F32),
            pltpu.SemaphoreType.DMA((44,)),
            pltpu.SemaphoreType.DMA((44,)),
            pltpu.SemaphoreType.DMA((7,)),
        ],
        compiler_params=pltpu.CompilerParams(
            collective_id=0, has_side_effects=True, vmem_limit_bytes=63 * 2**20
        ),
        name="relay",
    )(
        outgoing, returning, token_ids.reshape(2, 128), shared_basis, embed_table, norm_gain, value_weight,
        write_basis, head_logits,
    )
    next_out, next_ret, grad_write, grad_gain = pl.pallas_call(
        hand_over,
        out_shape=results,
        in_specs=[hbm] * 4,
        out_specs=(hbm,) * 4,
        scratch_shapes=[
            pltpu.VMEM((TOK, R), BF16),
            pltpu.VMEM((TOK, R), BF16),
            pltpu.VMEM((HD, R), F32),
            pltpu.VMEM((1, D), BF16),
            pltpu.SemaphoreType.DMA((8,)),
        ],
        compiler_params=pltpu.CompilerParams(vmem_limit_bytes=63 * 2**20),
        name="hand_over",
    )(*made)
    return (next_out, next_ret, grad_write[None], grad_gain)


def solution(mesh):
    placed = (
        P("section", None),
        P("section", None),
        P("section"),
        P("section", None),
        P(("tensor", "section"), None),
        P("section", None),
        P("section", None, "tensor"),
        P("section", "tensor", None),
        P("section", "tensor", None, None),
    )
    return jax.shard_map(
        shards,
        mesh=mesh,
        in_specs=placed,
        out_specs=(
            P("section", None),
            P("section", None),
            P("section", "tensor", None),
            P("section", None),
        ),
        check_vma=False,
    )
```

```python
import functools

import jax
import jax.numpy as jnp
from jax import lax
from jax.experimental import pallas as pl
from jax.experimental.pallas import tpu as pltpu
from jax.sharding import PartitionSpec as P

D = 8192
HD = 128
R = 512
TOK = 256
VOCAB = 65536
FEAT = 16
NS = 64
NT = 8
WIDTH = FEAT * NS
ROWS = TOK // NT
HALF = TOK // 2
CHIPS = 4
CHIP_W = 2 * WIDTH
NX = 4
NZ = 8
SIDE = NX * NZ
AT_X = 10
TURN_FIRST = 14
AT_ROWS = 44
AT_GRAD = 52
MESH = pl.DeviceIdType.MESH
F32 = jnp.float32
BF16 = jnp.bfloat16


def dot(a, b):
    return jnp.dot(a, b, preferred_element_type=F32)


def dot_nt(a, b):
    return lax.dot_general(a, b, (((1,), (1,)), ((), ())), preferred_element_type=F32)


def wait_bytes(view, sem):
    pltpu.make_async_copy(view, view, sem).wait()


def kernel(
    outgoing, returning, ids, basis_hbm, table_hbm, gain_hbm, weight, write_hbm, logits_hbm,
    next_out, next_ret, grad_write, grad_gain,
    basis_own, table, gain, write, logits,
    ids_raw, ids_all, ids_scalar, coef, cot, pieces, basis, w_all, table_t, stage,
    emb_out, emb_in, gv_own, gv_all, heads, gn, gn_in, res_c, res, ng, acc, v_out, v_in, st_out, st_in,
    in_out, in_in, g_hi, g_lo, att_own, att_in, rs_out, rs_in, rg_out, rg_in, ag, ag_in, ad, ad_in, gg_own, gg_in, gg_all, gw,
    send, recv, local,
):
    s = lax.axis_index("section")
    t = lax.axis_index("tensor")
    chip = t // 2
    core = lax.rem(t, 2)
    other = 1 - core
    y_lo = s // SIDE
    place = lax.rem(s, SIDE)
    z = lax.rem(s // NX, NZ)
    x = lax.rem(s, NX)

    def section_peer(k):
        return lax.rem(s + k, NS)

    def tensor_peer(k):
        return lax.rem(t + k, NT)

    def chip_peer(k):
        return lax.rem(chip + k, CHIPS)

    def fetch(src, dst, which):
        copy = pltpu.make_async_copy(src, dst, local.at[which])
        copy.start()
        return copy

    ids_copy = fetch(ids, ids_raw, 0)
    basis_copy = fetch(basis_hbm.at[:, pl.ds(pl.multiple_of(t * WIDTH, WIDTH), WIDTH)], basis_own, 1)
    table_copy = fetch(table_hbm, table, 2)
    logits_copy = fetch(logits_hbm.at[0, 0], logits, 3)
    write_copy = fetch(write_hbm.at[0], write.at[core], 4)
    gain_copy = fetch(gain_hbm.at[:, pl.ds(pl.multiple_of(chip * CHIP_W, CHIP_W), CHIP_W)], gain, 5)
    chip_rows = pl.ds(pl.multiple_of(chip * CHIP_W, CHIP_W), CHIP_W)
    own_cols = pl.ds(pl.multiple_of(chip * HD, HD), HD)
    w_copy = fetch(weight.at[0, chip_rows], w_all.at[:, own_cols], 6)

    barrier = pltpu.get_barrier_semaphore()

    def greet_section(k, c):
        pl.semaphore_signal(barrier, inc=1, device_id=(section_peer(k), t), device_id_type=MESH)
        return c

    def greet_tensor(k, c):
        pl.semaphore_signal(barrier, inc=1, device_id=(s, tensor_peer(k)), device_id_type=MESH)
        return c

    lax.fori_loop(1, NS, greet_section, 0)
    lax.fori_loop(1, NT, greet_tensor, 0)

    ids_copy.wait()
    own = ids_raw[...]
    ids_all[place, y_lo, 0:2, :] = (own >> 10) * 128 + (own & 127)
    ids_all[place, y_lo, 2:4, :] = (own >> 7) & 7
    basis_copy.wait()
    part = basis_own[...].astype(F32)
    pieces[x, z, y_lo] = jnp.concatenate([part[:, : WIDTH // 2], part[:, WIDTH // 2 :]], axis=0).astype(BF16)
    pl.semaphore_wait(barrier, NS + NT - 2)

    def push(src, dst, which, peer):
        pltpu.make_async_remote_copy(
            src_ref=src, dst_ref=dst, send_sem=send.at[which], recv_sem=recv.at[which],
            device_id=peer, device_id_type=MESH,
        ).start()

    def across(k):
        return (s, chip_peer(k) * 2 + core)

    partner = (s, chip * 2 + other)

    here = pl.ds(pl.multiple_of(core * HALF, HALF), HALF)
    there = pl.ds(pl.multiple_of(other * HALF, HALF), HALF)

    facing = (lax.rem(s + SIDE, NS), t)
    push(ids_all.at[place, y_lo], ids_all.at[place, y_lo], 19, facing)
    push(pieces.at[x, z, y_lo], pieces.at[x, z, y_lo], 3, facing)

    @pl.when(s > 0)
    def _():
        push(returning.at[here], cot.at[here], 2, (section_peer(NS - 1), t))

    @pl.when(s < NS - 1)
    def _():
        push(outgoing.at[here], coef.at[here], 1, (section_peer(1), t))


    table_copy.wait()

    def turn(b, c):
        tile = table[:, pl.ds(pl.multiple_of(b * 1024, 1024), 1024)]
        tile = jnp.concatenate([tile[:, v * 128 : (v + 1) * 128] for v in range(8)], axis=0)
        table_t[pl.ds(pl.multiple_of(b * 128, 128), 128), :] = tile.T.astype(F32)
        return c

    lax.fori_loop(0, TURN_FIRST, turn, 0)
    wait_bytes(ids_all.at[0, 0], recv.at[19])

    def send_ids(k, c):
        push(ids_all.at[place], ids_all.at[place], 0, (y_lo * SIDE + lax.rem(place + k, SIDE), t))
        return c

    lax.fori_loop(1, SIDE, send_ids, 0)
    for k in (2, 1, 3):
        rows = pl.ds(pl.multiple_of(chip_peer(k) * CHIP_W, CHIP_W), CHIP_W)
        push(weight.at[0, rows], w_all.at[:, own_cols], 4, across(k))
    wait_bytes(pieces.at[0, 0, 0], recv.at[3])

    def send_z(k, c):
        push(pieces.at[x, z], pieces.at[x, z], 11, (y_lo * SIDE + lax.rem(z + k, NZ) * NX + x, t))
        return c

    lax.fori_loop(1, NZ, send_z, 0)
    write_copy.wait()
    push(write.at[core], write.at[core], 18, partner)
    lax.fori_loop(TURN_FIRST, VOCAB // 1024, turn, 0)

    wait_bytes(ids_all.at[pl.ds(0, SIDE - 1)], recv.at[0])
    scalar_copy = fetch(ids_all, ids_scalar, 0)
    scalar_copy.wait()
    lane = lax.broadcasted_iota(jnp.int32, (8, 128), 1)
    sub = lax.broadcasted_iota(jnp.int32, (8, 128), 0)
    group = lane // FEAT

    def find(p, half):
        low = lax.rem(p, SIDE)
        high = p // SIDE
        groups = jnp.broadcast_to(ids_all[low, high, pl.ds(2 + half, 1), :], (8, 128))
        for j in range(0, 128, 16):
            found = [table_t[pl.ds(ids_scalar[low, high, half, j + i], 1), :] for i in range(16)]
            for i in range(16):
                stage[pl.ds(j + i, 1), :] = found[i]
        outs = []
        for q in range(2):
            place = jnp.take_along_axis(groups, 16 * group + 8 * q + sub, axis=1) * FEAT + lane % FEAT
            found = None
            for b in range(8):
                row = jnp.take_along_axis(stage[16 * b + 8 * q : 16 * b + 8 * q + 8, :], place, axis=1)
                found = row if found is None else jnp.where(group == b, row, found)
            outs.append(found)
        return jnp.concatenate(outs, axis=0).astype(BF16)


    def values_gradient():
        logits_copy.wait()
        query = lax.broadcasted_iota(jnp.int32, (TOK, TOK), 0)
        key = lax.broadcasted_iota(jnp.int32, (TOK, TOK), 1)
        scores = jnp.where(query >= key, logits[...].astype(F32), -1e30)
        expd = jnp.exp(scores - jnp.max(scores, axis=1, keepdims=True))
        soft = expd / jnp.sum(expd, axis=1, keepdims=True)
        heads[...] = soft.astype(BF16)
        to_turn = soft.T.astype(BF16)

        @pl.when(s < NS - 1)
        def _():
            wait_bytes(cot.at[here], recv.at[27])

        @pl.when(s == NS - 1)
        def _():
            last = pltpu.make_async_copy(returning, cot, local.at[0])
            last.start()
            last.wait()

        ga = dot_nt(cot[...], write[core]).astype(BF16)
        gv_own[...] = dot(to_turn, ga).astype(BF16)
        for j in (2, 1, 3):
            push(gv_own, gv_all.at[:, own_cols], 5, across(j))
        gv_all[:, own_cols] = gv_own[...]

    def look_up(k, c):
        p = section_peer(k)

        def one_half(half, cc):
            emb_out[p, pl.ds(pl.multiple_of(half * 16, 16), 16), :] = find(p, half)
            return cc

        lax.fori_loop(0, 2, one_half, 0)
        push(emb_out.at[p], emb_in.at[s], 6, (p, t))

        @pl.when(k == AT_X)
        def _():
            wait_bytes(pieces.at[0, pl.ds(0, NZ - 1)], recv.at[11])
            for j in (2, 1, 3):
                push(pieces.at[x], pieces.at[x], 12, (y_lo * SIDE + z * NX + lax.rem(x + j, NX), t))

        @pl.when(jnp.logical_and(k == AT_ROWS, s < NS - 1))
        def _():
            wait_bytes(cot.at[here], recv.at[2])
            push(cot.at[here], cot.at[here], 27, partner)

        @pl.when(jnp.logical_and(k == AT_ROWS, s > 0))
        def _():
            wait_bytes(coef.at[here], recv.at[1])
            push(coef.at[here], coef.at[here], 26, partner)

        @pl.when(k == AT_GRAD)
        def _():
            values_gradient()

        return c

    lax.fori_loop(1, NS, look_up, 0)

    def own_half(half, c):
        emb_in[s, pl.ds(pl.multiple_of(half * 16, 16), 16), :] = find(s, half)
        return c

    lax.fori_loop(0, 2, own_half, 0)

    wait_bytes(pieces.at[pl.ds(0, NX - 1)], recv.at[12])
    for lo in range(2):
        for zz in range(NZ):
            tile = pieces[:, zz, lo].astype(F32)
            for xx in range(NX):
                rows = slice((lo * NZ * NX + zz * NX + xx) * 8, (lo * NZ * NX + zz * NX + xx) * 8 + 8)
                if xx % 2 == 0:
                    pair = slice(rows.start, rows.start + 16)
                    for h in range(2):
                        both = jnp.concatenate([tile[xx, 8 * h : 8 * h + 8], tile[xx + 1, 8 * h : 8 * h + 8]], axis=0)
                        basis[core, pair, h * 512 : (h + 1) * 512] = both.astype(BF16)
    push(basis.at[core], basis.at[core], 13, partner)

    @pl.when(s > 0)
    def _():
        wait_bytes(coef.at[here], recv.at[26])

    @pl.when(s == 0)
    def _():
        coef[...] = jnp.zeros_like(coef)

    res_c[...] = dot(coef[...], basis[core])

    wait_bytes(emb_in.at[pl.ds(0, NS - 1)], recv.at[6])
    acc[...] = jnp.zeros_like(acc)
    lane16 = lax.broadcasted_iota(jnp.int32, (16, 128), 1) // FEAT

    def assemble(u, c):
        cols = pl.ds(pl.multiple_of(u * 128, 128), 128)
        for half in range(2):
            xs = [emb_in[8 * u + v, 16 * half : 16 * half + 16, :].astype(F32) for v in range(8)]
            for d in (4, 2, 1):
                low = (lane16 & d) == 0
                ys = list(xs)
                for v in range(8):
                    if v & d == 0:
                        a, b = xs[v], xs[v + d]
                        ys[v] = jnp.where(low, a, pltpu.roll(b, 16 * d, 1))
                        ys[v + d] = jnp.where(low, pltpu.roll(a, 128 - 16 * d, 1), b)
                xs = ys
            for b in range(8):
                rows = slice(128 * half + 16 * b, 128 * half + 16 * b + 16)
                r = (res_c[rows, cols] + xs[b]).astype(BF16)
                res[core, rows, cols] = r
                r = r.astype(F32)
                acc[rows, :] += r * r
        return c

    lax.fori_loop(0, WIDTH // 128, assemble, 0)
    push(res.at[core], res.at[core], 14, partner)
    st_out[...] = jnp.zeros_like(st_out)
    st_out[0:1, :] = jnp.sum(acc[...].T, axis=0, keepdims=True)

    def send_squares(k, c):
        push(st_out, st_in.at[t], 8, (s, tensor_peer(k)))
        return c

    lax.fori_loop(1, NT, send_squares, 0)
    st_in[t] = st_out[...]
    wait_bytes(st_in.at[pl.ds(0, NT - 1)], recv.at[8])
    total = st_in[0]
    for i in range(1, NT):
        total = total + st_in[i]
    inv_row = 1.0 / jnp.sqrt(total[0:1, :] / D + 1e-5)
    acc[...] = jnp.broadcast_to(inv_row, (128, TOK)).T
    gain_copy.wait()
    wait_bytes(res.at[0], recv.at[14])
    for i in range(2):

        def normalise(u, c):
            cols = pl.ds(pl.multiple_of(u * 128, 128), 128)
            wide = pl.ds(pl.multiple_of(i * WIDTH + u * 128, 128), 128)
            ng[:, wide] = (res[i, :, cols].astype(F32) * acc[...] * gain[:, wide]).astype(BF16)
            return c

        lax.fori_loop(0, WIDTH // 128, normalise, 0)

    w_copy.wait()
    wait_bytes(w_all.at[:, pl.ds(0, (CHIPS - 1) * HD)], recv.at[4])
    wait_bytes(gv_all.at[:, pl.ds(0, (CHIPS - 1) * HD)], recv.at[5])
    gn[...] = dot_nt(gv_all[...], w_all[...])
    push(gn.at[there], gn_in, 15, partner)
    inner = jnp.zeros((TOK, 128), F32)
    for u in range(CHIP_W // 128):
        cols = slice(u * 128, (u + 1) * 128)
        narrow = slice(u % 8 * 128, (u % 8 + 1) * 128)
        inner = inner + gn[:, cols] * gain[:, cols] * res[u // 8, :, narrow].astype(F32)
    in_out[...] = jnp.broadcast_to(jnp.sum(inner.T, axis=0, keepdims=True), (8, TOK))

    def send_inner(k, c):
        push(in_out, in_in.at[t], 16, (s, tensor_peer(k)))
        return c

    lax.fori_loop(1, NT, send_inner, 0)
    in_in[t] = in_out[...]

    for h in range(2):
        v = dot(ng[...], w_all[:, h * 256 : (h + 1) * 256]).astype(BF16)
        v_out[2 * h] = v[:, :HD]
        v_out[2 * h + 1] = v[:, HD:]
    for k in (2, 1, 3):
        push(v_out.at[chip_peer(k)], v_in.at[chip], 7, across(k))
    v_in[chip] = v_out[chip]

    wait_bytes(gn_in, recv.at[15])
    inv = acc[here, :]
    for u in range(CHIP_W // 128):
        cols = slice(u * 128, (u + 1) * 128)
        narrow = slice(u % 8 * 128, (u % 8 + 1) * 128)
        n = (gn[here, cols] + gn_in[:, cols]) * inv
        gn_in[:, cols] = n * gain[:, cols]
        gg_own[u : u + 1, :] = jnp.sum(n * res[u // 8, here, narrow].astype(F32), axis=0, keepdims=True)

    wait_bytes(v_in.at[pl.ds(0, CHIPS - 1)], recv.at[7])
    v = v_in[0].astype(F32)
    for i in range(1, CHIPS):
        v = v + v_in[i].astype(F32)
    attended = dot(heads[...], v.astype(BF16))
    att_own[...] = attended.astype(BF16)
    push(att_own.at[there], att_in, 17, partner)

    wait_bytes(in_in.at[pl.ds(0, NT - 1)], recv.at[16])
    total = in_in[0]
    for i in range(1, NT):
        total = total + in_in[i]
    acc[...] = jnp.broadcast_to(total[0:1, :], (128, TOK)).T
    back = acc[here, :] * inv * inv * inv / D
    for u in range(CHIP_W // 128):
        cols = slice(u * 128, (u + 1) * 128)
        narrow = slice(u % 8 * 128, (u % 8 + 1) * 128)
        g = gn_in[:, cols] - res[u // 8, here, narrow].astype(F32) * back
        upper = g.astype(BF16)
        g_hi[u // 8, :, narrow] = upper
        g_lo[u // 8, :, narrow] = (g - upper.astype(F32)).astype(BF16)
    wait_bytes(basis.at[0], recv.at[13])
    grad = dot_nt(g_hi[0], basis[0]) + dot_nt(g_lo[0], basis[0])
    grad = grad + (dot_nt(g_hi[1], basis[1]) + dot_nt(g_lo[1], basis[1]))
    grad = grad.astype(BF16)
    for i in range(CHIPS):
        rg_out[i] = grad[i * ROWS : (i + 1) * ROWS, :]
    for k in (2, 1, 3):
        push(rg_out.at[chip_peer(k)], rg_in.at[chip], 29, across(k))
    rg_in[chip] = rg_out[chip]

    wait_bytes(write.at[0], recv.at[18])
    delta = dot(att_own[here, :], write[core])
    wait_bytes(att_in, recv.at[17])
    delta = (delta + dot(att_in[...], write[other])).astype(BF16)
    for i in range(CHIPS):
        rs_out[i] = delta[i * ROWS : (i + 1) * ROWS, :]
    for k in (2, 1, 3):
        push(rs_out.at[chip_peer(k)], rs_in.at[chip], 9, across(k))
    rs_in[chip] = rs_out[chip]

    def send_gain(k, c):
        push(gg_own, gg_in.at[t], 10, (s, tensor_peer(k)))
        return c

    lax.fori_loop(1, NT, send_gain, 0)
    gg_in[t] = gg_own[...]
    mine = pl.ds(pl.multiple_of(core * HALF + chip * ROWS, ROWS), ROWS)

    def add_up(parts, base, to_all, to_core, first):
        total = base[mine, :].astype(F32)
        for i in range(CHIPS):
            total = total + parts[i].astype(F32)
        to_all[chip] = total.astype(BF16)
        for k in (2, 1, 3):
            push(to_all.at[chip], to_all.at[chip], first + k, across(k))
        push(to_all.at[chip], to_core.at[chip], first, partner)

    def forward(to_all, to_core, first):
        for k in (1, 3, 2):
            wait_bytes(to_all.at[0], recv.at[first + k])
            come = chip_peer(CHIPS - k)
            push(to_all.at[come], to_core.at[come], first + 3 + k, partner)

    def put(parts, whose, out, which):
        for i in range(CHIPS):
            rows = pl.ds(pl.multiple_of(whose * HALF + i * ROWS, ROWS), ROWS)
            pltpu.make_async_copy(parts.at[i], out.at[rows], local.at[which]).start()

    def collect(to_all, to_core, first, out, which):
        put(to_all, core, out, which)
        for k in (first, first + 4, first + 5, first + 6):
            wait_bytes(to_core.at[0], recv.at[k])
        put(to_core, other, out, which)

    wait_bytes(rg_in.at[pl.ds(0, CHIPS - 1)], recv.at[29])
    add_up(rg_in, cot, ag, ag_in, 30)
    wait_bytes(rs_in.at[pl.ds(0, CHIPS - 1)], recv.at[9])
    add_up(rs_in, coef, ad, ad_in, 37)
    gw[...] = dot(attended.T.astype(BF16), cot[...])
    gw_copy = fetch(gw, grad_write, 3)
    forward(ag, ag_in, 30)
    forward(ad, ad_in, 37)
    wait_bytes(gg_in.at[pl.ds(0, NT - 1)], recv.at[10])
    gg_all[...] = jnp.concatenate(
        [gg_in[2 * i, j : j + 1, :] + gg_in[2 * i + 1, j : j + 1, :] for i in range(CHIPS) for j in range(16)], axis=1
    ).astype(BF16)
    gg_copy = fetch(gg_all, grad_gain, 4)
    collect(ag, ag_in, 30, next_ret, 1)
    collect(ad, ad_in, 37, next_out, 2)
    wait_bytes(next_ret, local.at[1])
    wait_bytes(next_out, local.at[2])
    gw_copy.wait()
    gg_copy.wait()

    wait_bytes(ids_all.at[pl.ds(0, SIDE - 1)], send.at[0])
    wait_bytes(ids_all.at[0, 0], send.at[19])

    @pl.when(s < NS - 1)
    def _():
        wait_bytes(coef.at[here], send.at[1])
        wait_bytes(cot.at[here], send.at[27])

    @pl.when(s > 0)
    def _():
        wait_bytes(cot.at[here], send.at[2])
        wait_bytes(coef.at[here], send.at[26])

    wait_bytes(pieces.at[0, 0, 0], send.at[3])
    wait_bytes(w_all.at[:, pl.ds(0, (CHIPS - 1) * HD)], send.at[4])
    wait_bytes(gv_all.at[:, pl.ds(0, (CHIPS - 1) * HD)], send.at[5])
    wait_bytes(emb_in.at[pl.ds(0, NS - 1)], send.at[6])
    wait_bytes(v_in.at[pl.ds(0, CHIPS - 1)], send.at[7])
    wait_bytes(st_in.at[pl.ds(0, NT - 1)], send.at[8])
    wait_bytes(rs_in.at[pl.ds(0, CHIPS - 1)], send.at[9])
    wait_bytes(gg_in.at[pl.ds(0, NT - 1)], send.at[10])
    wait_bytes(pieces.at[0, pl.ds(0, NZ - 1)], send.at[11])
    wait_bytes(pieces.at[pl.ds(0, NX - 1)], send.at[12])
    wait_bytes(basis.at[0], send.at[13])
    wait_bytes(res.at[0], send.at[14])
    wait_bytes(gn_in, send.at[15])
    wait_bytes(in_in.at[pl.ds(0, NT - 1)], send.at[16])
    wait_bytes(att_in, send.at[17])
    wait_bytes(write.at[0], send.at[18])
    wait_bytes(rg_in.at[pl.ds(0, CHIPS - 1)], send.at[29])
    for which in range(30, 44):
        wait_bytes(ag_in.at[0], send.at[which])


def hand_over(a, b, c, d, a_out, b_out, c_out, d_out, a_here, b_here, c_here, d_here, sem):
    steps = ((a, a_here, a_out), (b, b_here, b_out), (c, c_here, c_out), (d, d_here, d_out))
    into = [pltpu.make_async_copy(src, here, sem.at[i]) for i, (src, here, _) in enumerate(steps)]
    out = [pltpu.make_async_copy(here, dst, sem.at[4 + i]) for i, (_, here, dst) in enumerate(steps)]
    for copy in into:
        copy.start()
    for first, second in zip(into, out):
        first.wait()
        second.start()
    for copy in out:
        copy.wait()


def shards(
    outgoing, returning, token_ids, shared_basis, embed_table, norm_gain, value_weight, write_basis, head_logits
):
    hbm = pl.BlockSpec(memory_space=pl.ANY)
    results = (
        jax.ShapeDtypeStruct((TOK, R), BF16),
        jax.ShapeDtypeStruct((TOK, R), BF16),
        jax.ShapeDtypeStruct((HD, R), F32),
        jax.ShapeDtypeStruct((1, D), BF16),
    )
    made = pl.pallas_call(
        kernel,
        out_shape=results,
        in_specs=[hbm] * 9,
        out_specs=(hbm,) * 4,
        scratch_shapes=[
            pltpu.VMEM((8, WIDTH), BF16),
            pltpu.VMEM((FEAT, VOCAB), BF16),
            pltpu.VMEM((1, CHIP_W), F32),
            pltpu.VMEM((2, HD, R), BF16),
            pltpu.VMEM((TOK, TOK), BF16),
            pltpu.VMEM((2, 128), jnp.int32),
            pltpu.VMEM((SIDE, 2, 4, 128), jnp.int32),
            pltpu.SMEM((SIDE, 2, 4, 128), jnp.int32),
            pltpu.VMEM((TOK, R), BF16),
            pltpu.VMEM((TOK, R), BF16),
            pltpu.VMEM((NX, NZ, 2, 16, WIDTH // 2), BF16),
            pltpu.VMEM((2, R, WIDTH), BF16),
            pltpu.VMEM((CHIP_W, CHIPS * HD), BF16),
            pltpu.VMEM((VOCAB // 8, 128), F32),
            pltpu.VMEM((128, 128), F32),
            pltpu.VMEM((NS, 32, 128), BF16),
            pltpu.VMEM((NS, 32, 128), BF16),
            pltpu.VMEM((TOK, HD), BF16),
            pltpu.VMEM((TOK, CHIPS * HD), BF16),
            pltpu.VMEM((TOK, TOK), BF16),
            pltpu.VMEM((TOK, CHIP_W), F32),
            pltpu.VMEM((HALF, CHIP_W), F32),
            pltpu.VMEM((TOK, WIDTH), F32),
            pltpu.VMEM((2, TOK, WIDTH), BF16),
            pltpu.VMEM((TOK, CHIP_W), BF16),
            pltpu.VMEM((TOK, 128), F32),
            pltpu.VMEM((CHIPS, TOK, HD), BF16),
            pltpu.VMEM((CHIPS, TOK, HD), BF16),
            pltpu.VMEM((8, TOK), F32),
            pltpu.VMEM((NT, 8, TOK), F32),
            pltpu.VMEM((8, TOK), F32),
            pltpu.VMEM((NT, 8, TOK), F32),
            pltpu.VMEM((2, HALF, WIDTH), BF16),
            pltpu.VMEM((2, HALF, WIDTH), BF16),
            pltpu.VMEM((TOK, HD), BF16),
            pltpu.VMEM((HALF, HD), BF16),
            pltpu.VMEM((CHIPS, ROWS, R), BF16),
            pltpu.VMEM((CHIPS, ROWS, R), BF16),
            pltpu.VMEM((CHIPS, ROWS, R), BF16),
            pltpu.VMEM((CHIPS, ROWS, R), BF16),
            pltpu.VMEM((CHIPS, ROWS, R), BF16),
            pltpu.VMEM((CHIPS, ROWS, R), BF16),
            pltpu.VMEM((CHIPS, ROWS, R), BF16),
            pltpu.VMEM((CHIPS, ROWS, R), BF16),
            pltpu.VMEM((16, 128), F32),
            pltpu.VMEM((NT, 16, 128), F32),
            pltpu.VMEM((1, D), BF16),
            pltpu.VMEM((HD, R), F32),
            pltpu.SemaphoreType.DMA((44,)),
            pltpu.SemaphoreType.DMA((44,)),
            pltpu.SemaphoreType.DMA((7,)),
        ],
        compiler_params=pltpu.CompilerParams(
            collective_id=0, has_side_effects=True, vmem_limit_bytes=63 * 2**20
        ),
        name="relay",
    )(
        outgoing, returning, token_ids.reshape(2, 128), shared_basis, embed_table, norm_gain, value_weight,
        write_basis, head_logits,
    )
    next_out, next_ret, grad_write, grad_gain = pl.pallas_call(
        hand_over,
        out_shape=results,
        in_specs=[hbm] * 4,
        out_specs=(hbm,) * 4,
        scratch_shapes=[
            pltpu.VMEM((TOK, R), BF16),
            pltpu.VMEM((TOK, R), BF16),
            pltpu.VMEM((HD, R), F32),
            pltpu.VMEM((1, D), BF16),
            pltpu.SemaphoreType.DMA((8,)),
        ],
        compiler_params=pltpu.CompilerParams(vmem_limit_bytes=63 * 2**20),
        name="hand_over",
    )(*made)
    return (next_out, next_ret, grad_write[None], grad_gain)


def solution(mesh):
    placed = (
        P("section", None),
        P("section", None),
        P("section"),
        P("section", None),
        P(("tensor", "section"), None),
        P("section", None),
        P("section", None, "tensor"),
        P("section", "tensor", None),
        P("section", "tensor", None, None),
    )
    return jax.shard_map(
        shards,
        mesh=mesh,
        in_specs=placed,
        out_specs=(
            P("section", None),
            P("section", None),
            P("section", "tensor", None),
            P("section", None),
        ),
        check_vma=False,
    )
```
